128 devices in a mesh: row: 8 (over y, core), col: 16 (over z, x).
Axes of the slice: x: 4, y: 4, z: 4, core: 2. Of those that a mesh axis runs over, the one named last changes fastest.
Arguments:
- block_x: float32 [64, 98304], P(None, ('row', 'col')), may hold values from -6 to 6
- block_p: float32 [64, 98304], P(None, ('row', 'col')), may hold values from -6 to 6
- tile_rows: int32 [8, 16, 576], P('row', 'col'), may hold values from 0 to 95, as said below
- tile_cols: int32 [8, 16, 576], P('row', 'col'), may hold values from 0 to 47, as said below
- tile_count: int32 [8, 16], P('row', 'col'), may hold values from 1 to 576, as said below
- tile_vals: bfloat16 [8, 16, 576, 128, 128], P('row', 'col'), may hold values from -0.125 to 0.125
Outputs:
- residual: float32 [64, 98304], P(None, ('row', 'col'))
- image_r: float32 [64, 98304], P(None, ('row', 'col'))
- gram_a: float32 [192, 192], replicated
- gram_b: float32 [192, 192], replicated
The draws below stay inside these ranges and needn't reach their ends.
Inputs may be any that keep to these rules, and one draw needn't show every extreme that they name: `tile_rows`: within one grid cell the live slots name distinct tiles, all with i <= j; slots at and beyond the cell's count are ignored. `tile_cols`: paired with tile_rows slot by slot. `tile_count`: some grid cell is full in every draw.
All inputs are finite; a program needn't handle non-finite values.
Results may differ from the reference program's by a relative error of at most 0.0035.
Values may be sent and summed in bfloat16 or wider, within the bound.
A program may use at most 128 MiB of HBM per device.

```python
import jax
import jax.numpy as jnp
from jax import lax

K = 64
TILE = 128
XB = 6
TILES_DEV = 576
NODES = 98304
N_ROW = 8
N_COL = 16


def tile_lists(key):
    row_span = N_COL * XB
    col_span = N_ROW * XB
    candidates = row_span * col_span
    position = jnp.arange(candidates, dtype=jnp.int32)
    local_row = position // col_span
    local_col = position % col_span
    device = jnp.arange(N_ROW * N_COL, dtype=jnp.int32)

    def one_cell(cell):
        grid_row = cell // N_COL
        grid_col = cell % N_COL
        block_row = grid_row * row_span + local_row
        block_col = local_col // XB * row_span + grid_col * XB + local_col % XB
        upper = (block_row <= block_col).astype(jnp.int32)
        shuffled = jax.random.permutation(jax.random.fold_in(key, cell), candidates)
        ranking = jnp.argsort(1 - upper[shuffled], stable=True)
        picked = shuffled[ranking][:TILES_DEV]
        return (local_row[picked], local_col[picked], jnp.sum(upper))
    rows_out, cols_out, upper_total = jax.vmap(one_cell)(device)
    target = TILES_DEV * (2 * (N_ROW - device // N_COL) - 1) // (2 * N_ROW - 1)
    jitter = jax.random.randint(jax.random.fold_in(key, 7001), (N_ROW * N_COL,), 0, 1 << 20) % (target // 4 + 1)
    counts = jnp.clip(target - jitter, 1, upper_total)
    busiest = jax.random.randint(jax.random.fold_in(key, 7002), (), 0, N_COL)
    counts = jnp.where(device == busiest, TILES_DEV, counts)
    counts = jnp.minimum(counts, upper_total).astype(jnp.int32)
    return (rows_out.reshape(N_ROW, N_COL, TILES_DEV).astype(jnp.int32), cols_out.reshape(N_ROW, N_COL, TILES_DEV).astype(jnp.int32), counts.reshape(N_ROW, N_COL))


def draw_tile_rows(key, part):
    return tile_lists(key)[0]


def draw_tile_cols(key, part):
    return tile_lists(key)[1]


def draw_tile_count(key, part):
    return tile_lists(key)[2]


def level_of(stream_key, dims, shards, smallest, top_value):
    level = 1.0
    for dim, shards_of in shards:
        steps = jax.random.uniform(jax.random.fold_in(jax.random.fold_in(stream_key, 6), dim), (shards_of,), jnp.float32, smallest / len(shards), top_value / len(shards))
        level = level * jnp.repeat(jnp.exp(steps), dims[dim] // shards_of).reshape((-1,) + (1,) * (len(dims) - 1 - dim))
    return level


def scatter_about(stream_key, shape, scale, bound, shards=(), held_as=jnp.bfloat16):
    result = scale * jax.random.normal(stream_key, shape, jnp.float32)
    if shards:
        result = result * level_of(stream_key, shape, shards, -0.22, 0.18)
    return jnp.clip(result, -bound, bound).astype(held_as)


def setup_inputs(seed: int = 0) -> dict:
    arg_keys = jax.random.split(jax.random.key(seed), 7)
    block_x = scatter_about(arg_keys[0], (K, NODES), 1.0, 6.0, ((1, 128),), jnp.float32)
    block_p = scatter_about(arg_keys[1], (K, NODES), 1.0, 6.0, ((1, 128),), jnp.float32)
    tile_rows = draw_tile_rows(jax.random.fold_in(arg_keys[6], 71), 0)
    tile_cols = draw_tile_cols(jax.random.fold_in(arg_keys[6], 71), 0)
    tile_count = draw_tile_count(jax.random.fold_in(arg_keys[6], 71), 0)
    tile_vals = scatter_about(arg_keys[5], (N_ROW, N_COL, TILES_DEV, TILE, TILE), ((TILE * TILES_DEV // XB) ** (0 - 0.5)), 0.125, ((0, 8), (1, 16)))
    return dict(block_x=block_x, block_p=block_p, tile_rows=tile_rows, tile_cols=tile_cols, tile_count=tile_count, tile_vals=tile_vals)


def graph_apply(vectors, tile_rows, tile_cols, tile_count, tile_vals):
    vec_width = vectors.shape[0]
    node_count = vectors.shape[1]
    block_total = node_count // TILE
    blocks = vectors.astype(jnp.float32).reshape(vec_width, block_total, TILE)
    row_span = N_COL * XB
    slots = jnp.arange(TILES_DEV, dtype=jnp.int32)

    def visit(totals, device):
        grid_row = device // N_COL
        grid_col = device % N_COL
        local_row = tile_rows[grid_row, grid_col]
        local_col = tile_cols[grid_row, grid_col]
        block_row = (grid_row * row_span + local_row).astype(jnp.int32)
        block_col = (local_col // XB * row_span + grid_col * XB + local_col % XB).astype(jnp.int32)
        live_slots = (slots < tile_count[grid_row, grid_col]).astype(jnp.float32)
        values = tile_vals[grid_row, grid_col].astype(jnp.float32) * live_slots[:, None, None]
        col_inputs = jnp.take(blocks, block_col, axis=1)
        row_inputs = jnp.take(blocks, block_row, axis=1)
        forward = jnp.einsum('wgb,gab->wga', col_inputs, values)
        backward = jnp.einsum('wga,gab->wgb', row_inputs, values)
        totals = totals.at[:, block_row].add(forward)
        totals = totals.at[:, block_col].add(backward)
        return (totals, None)
    start_totals = jnp.zeros((vec_width, block_total, TILE), jnp.float32)
    totals, unused = lax.scan(visit, start_totals, jnp.arange(N_ROW * N_COL, dtype=jnp.int32))
    return totals.reshape(vec_width, node_count)

def reference(block_x, block_p, tile_rows, tile_cols, tile_count, tile_vals):
    highest = lax.Precision.HIGHEST
    node_count = block_x.shape[1]
    gram_x = jnp.dot(block_x.astype(jnp.float32), block_x.T.astype(jnp.float32), precision=highest, preferred_element_type=jnp.float32) / node_count
    cholesky_factor = jnp.linalg.cholesky(gram_x)
    orthonormal = lax.linalg.triangular_solve(cholesky_factor, block_x, left_side=True, lower=True)
    ortho_low = orthonormal.astype(jnp.bfloat16)
    dir_low = block_p.astype(jnp.bfloat16)
    image_x = graph_apply(ortho_low, tile_rows, tile_cols, tile_count, tile_vals)
    image_p = graph_apply(dir_low, tile_rows, tile_cols, tile_count, tile_vals)
    rayleigh = jnp.dot(orthonormal.astype(jnp.float32), image_x.T.astype(jnp.float32), precision=highest, preferred_element_type=jnp.float32) / node_count
    residual = image_x - jnp.dot(rayleigh.T.astype(jnp.float32), orthonormal.astype(jnp.float32), precision=highest, preferred_element_type=jnp.float32)
    residual_low = residual.astype(jnp.bfloat16)
    image_r = graph_apply(residual_low, tile_rows, tile_cols, tile_count, tile_vals)
    basis = jnp.concatenate([orthonormal, residual, block_p], axis=0)
    images = jnp.concatenate([image_x, image_r, image_p], axis=0)
    gram_a = jnp.dot(basis.astype(jnp.float32), images.T.astype(jnp.float32), precision=highest, preferred_element_type=jnp.float32) / node_count
    gram_b = jnp.dot(basis.astype(jnp.float32), basis.T.astype(jnp.float32), precision=highest, preferred_element_type=jnp.float32) / node_count
    return (residual, image_r, gram_a, gram_b)
```

```python
import functools

import jax
import jax.numpy as jnp
from jax import lax
from jax.experimental import pallas as pl
from jax.experimental.pallas import tpu as pltpu
from jax.sharding import PartitionSpec as P

F32 = jnp.float32
BF16 = jnp.bfloat16
TILE = 128
HIGHEST = lax.Precision.HIGHEST
MESH = pl.DeviceIdType.MESH
VMEM_LIMIT = 56 * 2**20
GROUP = 48
UNROLL = 16
X_WIRE = F32
R_WIRE = BF16


def dot_nt(left, right):
    return lax.dot_general(
        left, right, (((1,), (1,)), ((), ())), precision=HIGHEST, preferred_element_type=F32
    )


def dot_tn(left, right):
    return lax.dot_general(
        left, right, (((0,), (0,)), ((), ())), precision=HIGHEST, preferred_element_type=F32
    )


def dot_nn(left, right):
    return lax.dot_general(
        left, right, (((1,), (0,)), ((), ())), precision=HIGHEST, preferred_element_type=F32
    )


class Line:
    def __init__(self, name, size):
        self.name, self.size = name, size
        self.me = lax.axis_index(name)

    def ahead(self, k):
        return lax.rem(self.me + k, self.size)

    def behind(self, k):
        return lax.rem(self.me + self.size - k, self.size)

    def greet(self, barrier):
        for k in range(1, self.size):
            pl.semaphore_signal(
                barrier, inc=1, device_id={self.name: self.ahead(k)}, device_id_type=MESH
            )

    def copies(self, source, target, send_sem, recv_sem):
        return [
            pltpu.make_async_remote_copy(
                src_ref=source(self.ahead(k)),
                dst_ref=target(self.me),
                send_sem=send_sem.at[k],
                recv_sem=recv_sem.at[k],
                device_id={self.name: self.ahead(k)},
                device_id_type=MESH,
            )
            for k in range(1, self.size)
        ]

    def arrivals(self, source, target, send_sem, recv_sem):
        return [
            pltpu.make_async_remote_copy(
                src_ref=source(self.ahead(k)),
                dst_ref=target(self.behind(k)),
                send_sem=send_sem.at[k],
                recv_sem=recv_sem.at[k],
                device_id={self.name: self.ahead(k)},
                device_id_type=MESH,
            )
            for k in range(1, self.size)
        ]


class Exchange:
    def __init__(self, line, source, target, sems):
        self.sent = line.copies(source, target, sems.at[0], sems.at[1])
        self.come = line.arrivals(source, target, sems.at[0], sems.at[1])

    def start(self):
        for c in self.sent:
            c.start()
        return self

    def wait_recv(self):
        for c in self.come:
            c.wait_recv()
        return self

    def wait_send(self):
        for c in self.sent:
            c.wait_send()
        return self


def enter(rows, cols):
    barrier = pltpu.get_barrier_semaphore()
    rows.greet(barrier)
    cols.greet(barrier)
    pl.semaphore_wait(barrier, rows.size + cols.size - 2)


def sum_slots(ref, count):
    total = ref[0]
    for j in range(1, count):
        total = total + ref[j]
    return total


def all_reduce(rows, cols, part, first, second, row_sems, col_sems):
    first[rows.me] = part
    one = Exchange(rows, lambda p: first.at[rows.me], lambda s: first.at[s], row_sems)
    one.start().wait_recv()
    second[cols.me] = sum_slots(first, rows.size)
    two = Exchange(cols, lambda p: second.at[cols.me], lambda s: second.at[s], col_sems)
    two.start().wait_recv()
    total = sum_slots(second, cols.size)
    one.wait_send()
    two.wait_send()
    return total


def factor(gram):
    k_width = gram.shape[0]
    row_id = lax.broadcasted_iota(jnp.int32, (k_width, k_width), 0)
    col_id = lax.broadcasted_iota(jnp.int32, (k_width, k_width), 1)
    eye = jnp.where(row_id == col_id, 1.0, 0.0).astype(F32)
    work = jnp.concatenate([gram, eye], axis=1)
    down = lax.broadcasted_iota(jnp.int32, (k_width, 2 * k_width), 0)
    pivots = []
    for k in range(k_width):
        pivot_row = work[k : k + 1, :]
        pivot = work[k : k + 1, k : k + 1]
        pivots.append(pivot)
        if k + 1 < k_width:
            ratio = work[:, k : k + 1] / pivot
            work = work - jnp.where(down > k, ratio * pivot_row, 0.0)
    scale = lax.rsqrt(jnp.concatenate(pivots, axis=0))
    return work[:, k_width:] * scale


def first_kernel(
    n_row, n_col, node_count, x_ref, p_ref, ortho_ref, vrow_ref, vcol_ref,
    low, first, second, ar_row, ar_col, p_row, p_col, x_row, x_col, own,
):
    rows, cols = Line("row", n_row), Line("col", n_col)
    k_width, mine = x_ref.shape
    blocks = mine // TILE
    enter(rows, cols)

    for b in range(blocks):
        low[b, k_width:, :] = p_ref[:, b * TILE : (b + 1) * TILE].astype(BF16)

    gram = dot_nt(x_ref[...], x_ref[...]) / node_count
    zero = jnp.zeros((k_width, TILE - k_width), F32)
    part = jnp.concatenate([gram, zero], axis=1)

    x_half, p_half = pl.ds(0, k_width), pl.ds(k_width, k_width)

    def gather(line, out, half, sems):
        return Exchange(
            line, lambda p: low.at[:, half, :], lambda s: out.at[s, :, half, :], sems
        )

    p_moves = [gather(cols, vrow_ref, p_half, p_col), gather(rows, vcol_ref, p_half, p_row)]
    x_moves = [gather(cols, vrow_ref, x_half, x_col), gather(rows, vcol_ref, x_half, x_row)]
    for m in p_moves:
        m.start()
    gram = all_reduce(rows, cols, part, first, second, ar_row, ar_col)[:, :k_width]
    ortho = dot_nn(factor(gram), x_ref[...])
    ortho_ref[...] = ortho
    for b in range(blocks):
        low[b, :k_width, :] = ortho[:, b * TILE : (b + 1) * TILE].astype(BF16)
    for m in x_moves:
        m.start()
    here = [
        pltpu.make_async_copy(low, vrow_ref.at[cols.me], own.at[0]),
        pltpu.make_async_copy(low, vcol_ref.at[rows.me], own.at[1]),
    ]
    for c in here:
        c.start()
    for m in p_moves + x_moves:
        m.wait_recv()
    for m in p_moves + x_moves:
        m.wait_send()
    for c in here:
        c.wait()


def apply_kernel(
    splits, rows_ref, cols_ref, count_ref, vrow_ref, vcol_ref, tile_ref, *rest
):
    outs, (row_acc, col_acc) = rest[:-2], rest[-2:]
    row_blocks, col_blocks = vrow_ref.shape[0], vcol_ref.shape[0]
    step = pl.program_id(0)

    @pl.when(step == 0)
    def _():
        row_acc[...] = jnp.zeros_like(row_acc)
        col_acc[...] = jnp.zeros_like(col_acc)

    count = count_ref[0]
    base = step * GROUP
    todo = jnp.clip(count - base, 0, GROUP)

    def body(turn, carry):
        for u in range(UNROLL):
            slot = turn * UNROLL + u
            live = base + slot < count
            a = rows_ref[base + slot]
            b = cols_ref[base + slot]
            tile = tile_ref[slot]
            forward = lax.dot_general(
                vcol_ref[b], tile, (((1,), (1,)), ((), ())), preferred_element_type=F32
            )
            row_acc[jnp.where(live, a, row_blocks)] += forward
            backward = lax.dot_general(
                vrow_ref[a], tile, (((1,), (0,)), ((), ())), preferred_element_type=F32
            )
            col_acc[jnp.where(live, b, col_blocks)] += backward
        return carry

    lax.fori_loop(0, (todo + UNROLL - 1) // UNROLL, body, 0)

    @pl.when(step == pl.num_programs(0) - 1)
    def _():
        at = 0
        for i, width in enumerate(splits):
            for out, acc, n in ((outs[2 * i], row_acc, row_blocks), (outs[2 * i + 1], col_acc, col_blocks)):
                out[...] = acc[:n, at : at + width, :].astype(out.dtype)
            at += width


def apply_graph(tile_rows, tile_cols, count, vrow, vcol, tile_vals, splits):
    width = vrow.shape[1]
    slots = tile_vals.shape[0]
    n_r, n_c = vrow.shape[0], vcol.shape[0]
    whole = lambda n, w: pl.BlockSpec((n, w, TILE), lambda g, *_: (0, 0, 0))
    out_shape, out_specs = [], []
    for w, wire in splits:
        for n in (n_r, n_c):
            out_shape.append(jax.ShapeDtypeStruct((n, w, TILE), wire))
            out_specs.append(whole(n, w))
    flops = 4 * slots * width * TILE * TILE
    return pl.pallas_call(
        functools.partial(apply_kernel, [w for w, _ in splits]),
        grid_spec=pltpu.PrefetchScalarGridSpec(
            num_scalar_prefetch=3,
            grid=(slots // GROUP,),
            in_specs=[
                whole(n_r, width),
                whole(n_c, width),
                pl.BlockSpec((GROUP, TILE, TILE), lambda g, *_: (g, 0, 0)),
            ],
            out_specs=out_specs,
            scratch_shapes=[
                pltpu.VMEM((n_r + 1, width, TILE), F32),
                pltpu.VMEM((n_c + 1, width, TILE), F32),
            ],
        ),
        out_shape=out_shape,
        compiler_params=pltpu.CompilerParams(vmem_limit_bytes=VMEM_LIMIT),
        cost_estimate=pl.CostEstimate(
            flops=flops, bytes_accessed=2 * slots * TILE * TILE, transcendentals=0
        ),
    )(tile_rows, tile_cols, count, vrow, vcol, tile_vals)


class Scatter:
    def __init__(self, rows, cols, by_row, by_col, row_in, col_in, sems, own):
        row_sems, col_sems = sems
        blocks = row_in.shape[1]
        self.row_in, self.col_in = row_in, col_in
        self.n_col, self.n_row = cols.size, rows.size
        part = lambda ref: lambda p: ref.at[pl.ds(p * blocks, blocks)]
        self.moves = [
            Exchange(cols, part(by_row), lambda s: row_in.at[s], col_sems),
            Exchange(rows, part(by_col), lambda s: col_in.at[s], row_sems),
        ]
        self.here = [
            pltpu.make_async_copy(part(by_row)(cols.me), row_in.at[cols.me], own.at[0]),
            pltpu.make_async_copy(part(by_col)(rows.me), col_in.at[rows.me], own.at[1]),
        ]

    def start(self):
        for m in self.moves + self.here:
            m.start()

    def finish(self, image_ref):
        for m in self.moves:
            m.wait_recv()
        for c in self.here:
            c.wait()
        for b in range(self.row_in.shape[1]):
            total = self.row_in[0, b].astype(F32)
            for j in range(1, self.n_col):
                total = total + self.row_in[j, b].astype(F32)
            for j in range(self.n_row):
                total = total + self.col_in[j, b].astype(F32)
            image_ref[:, b * TILE : (b + 1) * TILE] = total

    def wait_send(self):
        for m in self.moves:
            m.wait_send()


def middle_kernel(
    n_row, n_col, node_count, ortho_ref, xr_ref, xc_ref, pr_ref, pc_ref,
    residual_ref, image_x_ref, image_p_ref, vrow_ref, vcol_ref,
    xr_in, xc_in, pr_in, pc_in, low, first, second,
    x_row, x_col, p_row, p_col, ar_row, ar_col, g_row, g_col, own,
):
    rows, cols = Line("row", n_row), Line("col", n_col)
    k_width, mine = ortho_ref.shape
    blocks = mine // TILE
    enter(rows, cols)
    x_sum = Scatter(rows, cols, xr_ref, xc_ref, xr_in, xc_in, (x_row, x_col), own.at[0])
    p_sum = Scatter(rows, cols, pr_ref, pc_ref, pr_in, pc_in, (p_row, p_col), own.at[1])
    x_sum.start()
    x_sum.finish(image_x_ref)
    ortho = ortho_ref[...]
    part = dot_nt(ortho, image_x_ref[...]) / node_count
    zero = jnp.zeros((k_width, TILE - k_width), F32)
    part = jnp.concatenate([part, zero], axis=1)
    rayleigh = all_reduce(rows, cols, part, first, second, ar_row, ar_col)[:, :k_width]
    residual = image_x_ref[...] - dot_tn(rayleigh, ortho)
    residual_ref[...] = residual
    for b in range(blocks):
        low[b] = residual[:, b * TILE : (b + 1) * TILE].astype(BF16)
    gathers = [
        Exchange(cols, lambda p: low, lambda s: vrow_ref.at[s], g_col),
        Exchange(rows, lambda p: low, lambda s: vcol_ref.at[s], g_row),
    ]
    here = [
        pltpu.make_async_copy(low, vrow_ref.at[cols.me], own.at[2, 0]),
        pltpu.make_async_copy(low, vcol_ref.at[rows.me], own.at[2, 1]),
    ]
    for c in gathers + here:
        c.start()
    p_sum.start()
    for c in gathers:
        c.wait_recv()
    p_sum.finish(image_p_ref)
    for c in here:
        c.wait()
    for c in gathers + [x_sum, p_sum]:
        c.wait_send()


def last_kernel(
    n_row, n_col, node_count, ortho_ref, residual_ref, p_ref, image_x_ref, image_p_ref,
    rr_ref, rc_ref, image_r_ref, gram_a_ref, gram_b_ref,
    rr_in, rc_in, whole, done, first, second, r_row, r_col, s_row, s_col, g_row, own,
):
    rows, cols = Line("row", n_row), Line("col", n_col)
    k_width = ortho_ref.shape[0]
    full = 3 * k_width
    share = full // n_row
    enter(rows, cols)
    r_sum = Scatter(rows, cols, rr_ref, rc_ref, rr_in, rc_in, (r_row, r_col), own)
    r_sum.start()
    basis = jnp.concatenate([ortho_ref[...], residual_ref[...], p_ref[...]], axis=0)
    whole[:, full:] = dot_nt(basis, basis) / node_count
    r_sum.finish(image_r_ref)
    images = jnp.concatenate([image_x_ref[...], image_r_ref[...], image_p_ref[...]], axis=0)
    whole[:, :full] = dot_nt(basis, images) / node_count

    def mine(p):
        return pl.ds(pl.multiple_of(p * share, 8), share)

    first[rows.me] = whole[mine(rows.me), :]
    one = Exchange(rows, lambda p: whole.at[mine(p)], lambda s: first.at[s], s_row)
    one.start().wait_recv()
    second[cols.me] = sum_slots(first, n_row)
    two = Exchange(cols, lambda p: second.at[cols.me], lambda s: second.at[s], s_col)
    two.start().wait_recv()
    one.wait_send()
    done[mine(rows.me), :] = sum_slots(second, n_col)
    three = Exchange(
        rows, lambda p: done.at[mine(rows.me)], lambda s: done.at[mine(s)], g_row
    )
    three.start().wait_recv()
    gram_a_ref[...] = done[:, :full]
    gram_b_ref[...] = done[:, full:]
    two.wait_send()
    three.wait_send()
    r_sum.wait_send()


def per_device(block_x, block_p, tile_rows, tile_cols, tile_count, tile_vals):
    n_row, n_col = lax.axis_size("row"), lax.axis_size("col")
    k_width, mine = block_x.shape
    node_count = mine * n_row * n_col
    blocks = mine // TILE
    slots = tile_vals.shape[2]
    slot_rows = tile_rows.reshape(slots)
    slot_cols = tile_cols.reshape(slots)
    count = tile_count.reshape(1)
    vals = tile_vals.reshape(slots, TILE, TILE)
    vmem = pl.BlockSpec(memory_space=pltpu.VMEM)
    anywhere = pl.BlockSpec(memory_space=pl.ANY)
    row_sems = pltpu.SemaphoreType.DMA((2, n_row))
    col_sems = pltpu.SemaphoreType.DMA((2, n_col))
    shape = jax.ShapeDtypeStruct
    params = lambda i: pltpu.CompilerParams(
        collective_id=i, has_side_effects=True, vmem_limit_bytes=VMEM_LIMIT
    )
    local = shape((k_width, mine), F32)

    ortho, vrow, vcol = pl.pallas_call(
        functools.partial(first_kernel, n_row, n_col, node_count),
        in_specs=[vmem] * 2,
        out_specs=[vmem, anywhere, anywhere],
        out_shape=[
            local,
            shape((n_col, blocks, 2 * k_width, TILE), BF16),
            shape((n_row, blocks, 2 * k_width, TILE), BF16),
        ],
        scratch_shapes=[
            pltpu.VMEM((blocks, 2 * k_width, TILE), BF16),
            pltpu.VMEM((n_row, k_width, TILE), F32),
            pltpu.VMEM((n_col, k_width, TILE), F32),
            row_sems, col_sems, row_sems, col_sems, row_sems, col_sems,
            pltpu.SemaphoreType.DMA((2,)),
        ],
        compiler_params=params(0),
    )(block_x, block_p)

    def spread(v, n):
        return v.reshape(n * blocks, v.shape[2], TILE)

    xr, xc, pr, pc = apply_graph(
        slot_rows, slot_cols, count, spread(vrow, n_col), spread(vcol, n_row), vals,
        ((k_width, X_WIRE), (k_width, R_WIRE)),
    )

    residual, image_x, image_p, vrow, vcol = pl.pallas_call(
        functools.partial(middle_kernel, n_row, n_col, node_count),
        in_specs=[vmem] + [anywhere] * 4,
        out_specs=[vmem, vmem, vmem, anywhere, anywhere],
        out_shape=[
            local, local, local,
            shape((n_col, blocks, k_width, TILE), BF16),
            shape((n_row, blocks, k_width, TILE), BF16),
        ],
        scratch_shapes=[
            pltpu.VMEM((n_col, blocks, k_width, TILE), X_WIRE),
            pltpu.VMEM((n_row, blocks, k_width, TILE), X_WIRE),
            pltpu.VMEM((n_col, blocks, k_width, TILE), R_WIRE),
            pltpu.VMEM((n_row, blocks, k_width, TILE), R_WIRE),
            pltpu.VMEM((blocks, k_width, TILE), BF16),
            pltpu.VMEM((n_row, k_width, TILE), F32),
            pltpu.VMEM((n_col, k_width, TILE), F32),
            row_sems, col_sems, row_sems, col_sems, row_sems, col_sems, row_sems, col_sems,
            pltpu.SemaphoreType.DMA((3, 2)),
        ],
        compiler_params=params(1),
    )(ortho, xr, xc, pr, pc)

    rr, rc = apply_graph(
        slot_rows, slot_cols, count, spread(vrow, n_col), spread(vcol, n_row), vals,
        ((k_width, R_WIRE),),
    )

    full = 3 * k_width
    image_r, gram_a, gram_b = pl.pallas_call(
        functools.partial(last_kernel, n_row, n_col, node_count),
        in_specs=[vmem] * 5 + [anywhere] * 2,
        out_specs=[vmem] * 3,
        out_shape=[local, shape((full, full), F32), shape((full, full), F32)],
        scratch_shapes=[
            pltpu.VMEM((n_col, blocks, k_width, TILE), R_WIRE),
            pltpu.VMEM((n_row, blocks, k_width, TILE), R_WIRE),
            pltpu.VMEM((full, 2 * full), F32),
            pltpu.VMEM((full, 2 * full), F32),
            pltpu.VMEM((n_row, full // n_row, 2 * full), F32),
            pltpu.VMEM((n_col, full // n_row, 2 * full), F32),
            row_sems, col_sems, row_sems, col_sems, row_sems,
            pltpu.SemaphoreType.DMA((2,)),
        ],
        compiler_params=params(2),
    )(ortho, residual, block_p, image_x, image_p, rr, rc)
    return residual, image_r, gram_a, gram_b


def solution(mesh):
    in_specs = (
        P(None, ("row", "col")),
        P(None, ("row", "col")),
        P("row", "col", None),
        P("row", "col", None),
        P("row", "col"),
        P("row", "col", None, None, None),
    )
    out_specs = (P(None, ("row", "col")), P(None, ("row", "col")), P(), P())
    return jax.shard_map(
        per_device, mesh=mesh, in_specs=in_specs, out_specs=out_specs, check_vma=False
    )
```

```python
import functools

import jax
import jax.numpy as jnp
from jax import lax
from jax.experimental import pallas as pl
from jax.experimental.pallas import tpu as pltpu
from jax.sharding import PartitionSpec as P

F32 = jnp.float32
BF16 = jnp.bfloat16
TILE = 128
HIGHEST = lax.Precision.HIGHEST
MESH = pl.DeviceIdType.MESH
VMEM_LIMIT = 56 * 2**20
GROUP = 48
SIDE = 4
HALF = 3
SPARE = 16
TOP = 32700.0


def dot_nt(left, right):
    return lax.dot_general(
        left, right, (((1,), (1,)), ((), ())), precision=HIGHEST, preferred_element_type=F32
    )


def dot_tn(left, right):
    return lax.dot_general(
        left, right, (((0,), (0,)), ((), ())), precision=HIGHEST, preferred_element_type=F32
    )


def dot_nn(left, right):
    return lax.dot_general(
        left, right, (((1,), (0,)), ((), ())), precision=HIGHEST, preferred_element_type=F32
    )


class Line:
    def __init__(self, name, size):
        self.name, self.size = name, size
        self.me = lax.axis_index(name)

    def ahead(self, k):
        return lax.rem(self.me + k, self.size)

    def behind(self, k):
        return lax.rem(self.me + self.size - k, self.size)

    def greet(self, barrier):
        for k in range(1, self.size):
            pl.semaphore_signal(
                barrier, inc=1, device_id={self.name: self.ahead(k)}, device_id_type=MESH
            )

    def copies(self, source, target, send_sem, recv_sem):
        return [
            pltpu.make_async_remote_copy(
                src_ref=source(self.ahead(k)),
                dst_ref=target(self.me),
                send_sem=send_sem.at[k],
                recv_sem=recv_sem.at[k],
                device_id={self.name: self.ahead(k)},
                device_id_type=MESH,
            )
            for k in range(1, self.size)
        ]

    def arrivals(self, source, target, send_sem, recv_sem):
        return [
            pltpu.make_async_remote_copy(
                src_ref=source(self.ahead(k)),
                dst_ref=target(self.behind(k)),
                send_sem=send_sem.at[k],
                recv_sem=recv_sem.at[k],
                device_id={self.name: self.ahead(k)},
                device_id_type=MESH,
            )
            for k in range(1, self.size)
        ]


class Exchange:
    def __init__(self, line, source, target, sems):
        self.sent = line.copies(source, target, sems.at[0], sems.at[1])
        self.come = line.arrivals(source, target, sems.at[0], sems.at[1])

    def start(self):
        for c in self.sent:
            c.start()
        return self

    def wait_recv(self):
        for c in self.come:
            c.wait_recv()
        return self

    def wait_send(self):
        for c in self.sent:
            c.wait_send()
        return self


def pack(parts, ref):
    width = parts[0].shape[0]
    most = jnp.abs(parts[0])
    for part in parts[1:]:
        most = jnp.maximum(most, jnp.abs(part))
    most = jnp.maximum(jnp.max(most, axis=1, keepdims=True), 1e-30)
    power = jnp.clip(jnp.ceil(jnp.log2(most)), -100.0, 126.0)
    up = jnp.exp2(-power) * TOP
    for i, part in enumerate(parts):
        ref[i * width : (i + 1) * width, :] = jnp.round(part * up).astype(jnp.int32).astype(jnp.int16)
    down = lax.broadcasted_iota(jnp.int32, (width, TILE), 0)
    across = lax.broadcasted_iota(jnp.int32, (width, TILE), 1)
    line = jnp.sum(jnp.where(down == across, power, 0.0), axis=0, keepdims=True)
    line = jnp.broadcast_to(line, (SPARE, TILE))
    ref[len(parts) * width :, :] = line.astype(jnp.int32).astype(jnp.int16)


def unpack(ref, count, width):
    line = ref[count * width :, :].astype(jnp.int32).astype(F32)[:1]
    down = lax.broadcasted_iota(jnp.int32, (width, TILE), 0)
    across = lax.broadcasted_iota(jnp.int32, (width, TILE), 1)
    power = jnp.sum(jnp.where(down == across, line, 0.0), axis=1, keepdims=True)
    step = jnp.exp2(power) * (1.0 / TOP)
    return [
        ref[i * width : (i + 1) * width, :].astype(jnp.int32).astype(F32) * step
        for i in range(count)
    ]


def add_lists(lists):
    return [functools.reduce(lambda a, b: a + b, parts) for parts in zip(*lists)]


class Plane:
    def __init__(self, cols):
        self.spot = (cols.me // SIDE, lax.rem(cols.me, SIDE))

    def axes(self, half):
        return (self.spot[0], self.spot[1]) if half == 0 else (self.spot[1], self.spot[0])

    def index(self, half, first, second):
        first, second = lax.rem(first, SIDE), lax.rem(second, SIDE)
        return first * SIDE + second if half == 0 else second * SIDE + first

    def copy(self, source, target, sems, at, device):
        return pltpu.make_async_remote_copy(
            src_ref=source,
            dst_ref=target,
            send_sem=sems.at[(0, *at)],
            recv_sem=sems.at[(1, *at)],
            device_id={"col": device},
            device_id_type=MESH,
        )


class PlaneGather:
    def __init__(self, plane, mine, slot, sems):
        self.plane, self.mine, self.slot, self.sems = plane, mine, slot, sems
        self.sent = []

    def send(self, source, owner, half, at, device):
        c = self.plane.copy(source, self.slot(owner, half), self.sems, at, device)
        c.start()
        self.sent.append(c)

    def arrived(self, owner, half, at):
        _, device = self.place(half, 1, 0)
        self.plane.copy(self.mine(half), self.slot(owner, half), self.sems, at, device).wait_recv()

    def place(self, half, first, second):
        f, s = self.plane.axes(half)
        return (
            self.plane.index(half, f + SIDE - first, s + SIDE - second),
            self.plane.index(half, f + first, s + second),
        )

    def start(self):
        for half in (0, 1):
            me, _ = self.place(half, 0, 0)
            for k in range(1, SIDE):
                self.send(self.mine(half), me, half, (half, k, 0), self.place(half, k, 0)[1])
        for half in (0, 1):
            me, _ = self.place(half, 0, 0)
            for k in range(1, SIDE):
                self.send(self.mine(half), me, half, (half, 0, k), self.place(half, 0, k)[1])

    def forward(self):
        for i in (1, 3, 2):
            for half in (0, 1):
                owner, _ = self.place(half, i, 0)
                self.arrived(owner, half, (half, i, 0))
                for k in range(1, SIDE):
                    self.send(
                        self.slot(owner, half), owner, half, (half, i, k), self.place(half, 0, k)[1]
                    )

    def wait_recv(self):
        for i in range(SIDE):
            for k in range(1, SIDE):
                for half in (0, 1):
                    self.arrived(self.place(half, i, k)[0], half, (half, i, k))

    def wait_send(self):
        for c in self.sent:
            c.wait_send()


class PlaneSum:
    def __init__(self, plane, packed, first_in, second_in, second_out, sems1, sems2, own):
        self.plane, self.packed = plane, packed
        self.first_in, self.second_in, self.second_out = first_in, second_in, second_out
        self.sems1, self.sems2 = sems1, sems2
        self.own = [
            pltpu.make_async_copy(
                packed.at[h, pl.ds(plane.axes(h)[0] * SIDE, SIDE)], first_in.at[h, 0], own.at[h]
            )
            for h in (0, 1)
        ]
        self.sent = []

    def hop(self, half, k, j):
        f, s = self.plane.axes(half)
        return self.plane.copy(
            self.packed.at[half, lax.rem(f + k, SIDE) * SIDE + j],
            self.first_in.at[half, k, j],
            self.sems1,
            (half, k, j),
            self.plane.index(half, f + k, s),
        )

    def hop2(self, half, k):
        f, s = self.plane.axes(half)
        return self.plane.copy(
            self.second_out.at[half, k],
            self.second_in.at[half, k],
            self.sems2,
            (half, k),
            self.plane.index(half, f, s + k),
        )

    def start(self):
        for n in (2, 1, 3, 0):
            for half in (0, 1):
                for k in (2, 1, 3):
                    c = self.hop(half, k, self.turn(half, n))
                    c.start()
                    self.sent.append(c)
        for c in self.own:
            c.start()

    def turn(self, half, n):
        return lax.rem(self.plane.axes(half)[1] + n, SIDE)

    def gathered(self, half, k, width):
        j = self.turn(half, k)
        for i in range(1, SIDE):
            self.hop(half, i, j).wait_recv()
        return add_lists(
            [unpack(self.first_in.at[half, i, j], HALF, width) for i in range(SIDE)]
        )

    def pass_on(self, width):
        for c in self.own:
            c.wait()
        for k in (2, 1, 3):
            for half in (0, 1):
                pack(self.gathered(half, k, width), self.second_out.at[half, k])
                c = self.hop2(half, k)
                c.start()
                self.sent.append(c)

    def finish(self, width):
        mine = [self.gathered(half, 0, width) for half in (0, 1)]
        blocks = []
        for half in (0, 1):
            parts = [mine[half]]
            for k in (2, 1, 3):
                self.hop2(half, k).wait_recv()
                parts.append(unpack(self.second_in.at[half, k], HALF, width))
            blocks += add_lists(parts)
        return blocks

    def wait_send(self):
        for c in self.sent:
            c.wait_send()


class RowSum:
    def __init__(self, rows, packed, inbox, sems, own):
        self.rows, self.inbox = rows, inbox
        self.move = Exchange(rows, lambda p: packed.at[p], lambda s: inbox.at[s], sems)
        self.own = pltpu.make_async_copy(packed.at[rows.me], inbox.at[rows.me], own)

    def start(self):
        self.move.start()
        self.own.start()

    def finish(self, count, width):
        self.own.wait()
        self.move.wait_recv()
        return add_lists([unpack(self.inbox.at[j], count, width) for j in range(self.rows.size)])

    def wait_send(self):
        self.move.wait_send()


def enter(rows, cols):
    barrier = pltpu.get_barrier_semaphore()
    rows.greet(barrier)
    cols.greet(barrier)
    pl.semaphore_wait(barrier, rows.size + cols.size - 2)


def sum_slots(ref, count):
    total = ref[0]
    for j in range(1, count):
        total = total + ref[j]
    return total


def all_reduce(rows, cols, part, first, second, row_sems, col_sems, between=None):
    half = part.shape[0] // 2
    first[rows.me] = jnp.concatenate([part[:half], part[half:]], axis=1)
    one = Exchange(rows, lambda p: first.at[rows.me], lambda s: first.at[s], row_sems)
    one.start().wait_recv()
    second[cols.me] = sum_slots(first, rows.size)
    two = Exchange(cols, lambda p: second.at[cols.me], lambda s: second.at[s], col_sems)
    two.start()
    if between is not None:
        between()
    two.wait_recv()
    total = sum_slots(second, cols.size)
    one.wait_send()
    two.wait_send()
    return jnp.concatenate([total[:, : 2 * half], total[:, 2 * half :]], axis=0)


def factor(gram):
    k_width = gram.shape[0]
    row_id = lax.broadcasted_iota(jnp.int32, (k_width, k_width), 0)
    col_id = lax.broadcasted_iota(jnp.int32, (k_width, k_width), 1)
    eye = jnp.where(row_id == col_id, 1.0, 0.0).astype(F32)
    work = jnp.concatenate([gram, eye], axis=1)
    down = lax.broadcasted_iota(jnp.int32, (k_width, 2 * k_width), 0)
    pivots = []
    for k in range(k_width):
        pivot_row = work[k : k + 1, :]
        pivot = work[k : k + 1, k : k + 1]
        pivots.append(pivot)
        if k + 1 < k_width:
            ratio = work[:, k : k + 1]
            work = work - jnp.where(down > k, ratio * (pivot_row * (1.0 / pivot)), 0.0)
    scale = lax.rsqrt(jnp.concatenate(pivots, axis=0))
    return work[:, k_width:] * scale


def first_kernel(
    n_row, n_col, node_count, x_ref, p_ref, ortho_ref, vrow_ref, vcol_ref,
    low, first, second, ar_row, ar_col, p_row, p_plane, x_row, x_plane, own,
):
    rows, cols = Line("row", n_row), Line("col", n_col)
    plane = Plane(cols)
    k_width, mine = x_ref.shape
    blocks = mine // TILE
    enter(rows, cols)
    for b in range(blocks):
        low[b, k_width:, :] = p_ref[:, b * TILE : (b + 1) * TILE].astype(BF16)
    part = dot_nt(x_ref[...], x_ref[...]) / node_count

    def gathers(band, row_sems, plane_sems):
        across = PlaneGather(
            plane,
            lambda h: low.at[pl.ds(h * HALF, HALF), band, :],
            lambda owner, h: vrow_ref.at[owner, pl.ds(h * HALF, HALF), band, :],
            plane_sems,
        )
        along = Exchange(
            rows, lambda p: low.at[:, band, :], lambda s: vcol_ref.at[s, :, band, :], row_sems
        )
        return across, along

    p_across, p_along = gathers(pl.ds(k_width, k_width), p_row, p_plane)
    x_across, x_along = gathers(pl.ds(0, k_width), x_row, x_plane)

    def give_p():
        p_across.start()
        p_along.start()

    gram = all_reduce(rows, cols, part, first, second, ar_row, ar_col, give_p)
    p_across.forward()
    ortho = dot_nn(factor(gram), x_ref[...])
    ortho_ref[...] = ortho
    for b in range(blocks):
        low[b, :k_width, :] = ortho[:, b * TILE : (b + 1) * TILE].astype(BF16)
    x_across.start()
    x_along.start()
    here = [
        pltpu.make_async_copy(low, vrow_ref.at[cols.me], own.at[0]),
        pltpu.make_async_copy(low, vcol_ref.at[rows.me], own.at[1]),
    ]
    for c in here:
        c.start()
    x_across.forward()
    moves = (p_across, p_along, x_across, x_along)
    for m in moves:
        m.wait_recv()
    for m in moves:
        m.wait_send()
    for c in here:
        c.wait()


def times(left, right, right_dim):
    return lax.dot_general(
        left, right, (((1,), (right_dim,)), ((), ())), preferred_element_type=F32
    )


def apply_kernel(
    k_width, rows_ref, cols_ref, count_ref, vrow_ref, vcol_ref, tile_ref, *rest
):
    n_out = (len(rest) - 8) // 2
    outs, boxes = rest[:n_out], rest[n_out : 2 * n_out]
    vrow, vcol, tiles, row_acc, col_acc, tile_sems, in_sems, out_sems = rest[2 * n_out :]
    row_blocks, width, _ = vrow.shape
    col_blocks = vcol.shape[0]
    count = count_ref[0, 0]
    groups = (count + GROUP - 1) // GROUP

    def tile_copy(g):
        part = pl.ds(g * GROUP, GROUP)
        return pltpu.make_async_copy(tile_ref.at[part], tiles.at[part], tile_sems.at[g])

    def start_copy(g, carry):
        tile_copy(g).start()
        return carry

    inputs = [
        pltpu.make_async_copy(vcol_ref, vcol, in_sems.at[0]),
        pltpu.make_async_copy(vrow_ref, vrow, in_sems.at[1]),
    ]
    tile_copy(0).start()
    for c in inputs:
        c.start()
    lax.fori_loop(1, groups, start_copy, 0)
    row_acc[...] = jnp.zeros_like(row_acc)
    col_acc[...] = jnp.zeros_like(col_acc)
    for c in inputs:
        c.wait()

    def place(slot):
        live = slot < count
        a, b = rows_ref[0, 0, slot], cols_ref[0, 0, slot]
        return a, b, jnp.where(live, a, row_blocks), jnp.where(live, b, col_blocks)

    def single(slot):
        a, b, to_row, to_col = place(slot)
        tile = tiles[slot]
        row_acc[to_row] += times(vcol[b], tile, 1)
        col_acc[to_col] += times(vrow[a], tile, 0)

    def pair(slot):
        a, b, to_row, to_col = place(slot)
        a2, b2, to_row2, to_col2 = place(slot + 1)
        tile, tile2 = tiles[slot], tiles[slot + 1]
        none = jnp.zeros((width, TILE), BF16)

        def beside(u, v):
            return jnp.concatenate(
                [jnp.concatenate([u, none], axis=1), jnp.concatenate([none, v], axis=1)], axis=0
            )

        forward = times(beside(vcol[b], vcol[b2]), jnp.concatenate([tile, tile2], axis=1), 1)
        row_acc[to_row] += forward[:width]
        row_acc[to_row2] += forward[width:]
        backward = times(beside(vrow[a], vrow[a2]), jnp.concatenate([tile, tile2], axis=0), 0)
        col_acc[to_col] += backward[:width]
        col_acc[to_col2] += backward[width:]

    def group(g, carry):
        tile_copy(g).wait()
        if width < TILE:
            for u in range(0, GROUP, 2):
                pair(g * GROUP + u)
        else:
            for u in range(GROUP):
                single(g * GROUP + u)
        return carry

    lax.fori_loop(0, groups, group, 0)

    row_box, col_box = boxes[:2]
    n_row, n_col = col_box.shape[0], row_box.shape[1]
    blocks = row_blocks // n_col

    def pack_row(c, carry):
        for half in (0, 1):
            at = c if half == 0 else lax.rem(c, SIDE) * SIDE + c // SIDE
            parts = [row_acc[c * blocks + half * HALF + i, :k_width, :] for i in range(HALF)]
            pack(parts, row_box.at[half, at])
        return carry

    def pack_col(r, carry):
        pack([col_acc[r * blocks + i, :k_width, :] for i in range(blocks)], col_box.at[r])
        return carry

    results = [
        pltpu.make_async_copy(box, out, out_sems.at[i]) for i, (box, out) in enumerate(zip(boxes, outs))
    ]
    lax.fori_loop(0, n_col, pack_row, 0)
    results[0].start()
    lax.fori_loop(0, n_row, pack_col, 0)
    results[1].start()
    for i in range(2, n_out):
        acc, n = ((row_acc, row_blocks), (col_acc, col_blocks))[i - 2]
        boxes[i][...] = acc[:n, k_width:, :].astype(boxes[i].dtype)
        results[i].start()
    for c in results:
        c.wait()


def apply_graph(tile_rows, tile_cols, count, vrow, vcol, vals, k_width):
    n_col, blocks, width, _ = vrow.shape
    n_row = vcol.shape[0]
    slots = vals.shape[0]
    row_blocks, col_blocks = n_col * blocks, n_row * blocks
    smem = pl.BlockSpec(memory_space=pltpu.SMEM)
    anywhere = pl.BlockSpec(memory_space=pl.ANY)
    shape = jax.ShapeDtypeStruct
    out_shape = [
        shape((2, n_col, HALF * k_width + SPARE, TILE), jnp.int16),
        shape((n_row, blocks * k_width + SPARE, TILE), jnp.int16),
    ]
    if width > k_width:
        out_shape += [shape((n, width - k_width, TILE), BF16) for n in (row_blocks, col_blocks)]
    return pl.pallas_call(
        functools.partial(apply_kernel, k_width),
        in_specs=[smem] * 3 + [anywhere] * 3,
        out_specs=[anywhere] * len(out_shape),
        out_shape=out_shape,
        scratch_shapes=[
            *[pltpu.VMEM(o.shape, o.dtype) for o in out_shape],
            pltpu.VMEM((row_blocks, width, TILE), BF16),
            pltpu.VMEM((col_blocks, width, TILE), BF16),
            pltpu.VMEM((slots, TILE, TILE), BF16),
            pltpu.VMEM((row_blocks + 1, width, TILE), F32),
            pltpu.VMEM((col_blocks + 1, width, TILE), F32),
            pltpu.SemaphoreType.DMA((slots // GROUP,)),
            pltpu.SemaphoreType.DMA((2,)),
            pltpu.SemaphoreType.DMA((len(out_shape),)),
        ],
        compiler_params=pltpu.CompilerParams(vmem_limit_bytes=VMEM_LIMIT),
        cost_estimate=pl.CostEstimate(
            flops=16 * slots * width * TILE * TILE,
            bytes_accessed=2 * slots * TILE * TILE,
            transcendentals=0,
        ),
    )(
        tile_rows, tile_cols, count,
        vrow.reshape(row_blocks, width, TILE), vcol.reshape(col_blocks, width, TILE), vals,
    )


def middle_kernel(
    n_row, n_col, node_count, ortho_ref, xr_ref, xc_ref, pc_ref,
    residual_ref, image_x_ref, vrow_ref, vcol_ref, p_box_ref,
    first_in, second_in, second_out, inbox, low, first, second,
    s1, s2, s_row, ar_row, ar_col, g_row, g_plane, p_row, own,
):
    rows, cols = Line("row", n_row), Line("col", n_col)
    plane = Plane(cols)
    k_width, mine = ortho_ref.shape
    blocks = mine // TILE
    enter(rows, cols)
    across = PlaneSum(plane, xr_ref, first_in, second_in, second_out, s1, s2, own)
    along = RowSum(rows, xc_ref, inbox, s_row, own.at[2])
    across.start()
    along.start()
    across.pass_on(k_width)
    from_rows = along.finish(blocks, k_width)
    images = add_lists([across.finish(k_width), from_rows])
    image = jnp.concatenate(images, axis=1)
    image_x_ref[...] = image
    ortho = ortho_ref[...]
    part = dot_nt(ortho, image) / node_count
    p_along = Exchange(rows, lambda p: pc_ref.at[p], lambda s: p_box_ref.at[s], p_row)
    rayleigh = all_reduce(rows, cols, part, first, second, ar_row, ar_col, p_along.start)
    residual = image_x_ref[...] - dot_tn(rayleigh, ortho)
    residual_ref[...] = residual
    for b in range(blocks):
        low[b] = residual[:, b * TILE : (b + 1) * TILE].astype(BF16)
    g_across = PlaneGather(
        plane,
        lambda h: low.at[pl.ds(h * HALF, HALF)],
        lambda owner, h: vrow_ref.at[owner, pl.ds(h * HALF, HALF)],
        g_plane,
    )
    g_along = Exchange(rows, lambda p: low, lambda s: vcol_ref.at[s], g_row)
    g_across.start()
    g_along.start()
    here = [
        pltpu.make_async_copy(low, vrow_ref.at[cols.me], own.at[3]),
        pltpu.make_async_copy(low, vcol_ref.at[rows.me], own.at[4]),
        pltpu.make_async_copy(pc_ref.at[rows.me], p_box_ref.at[rows.me], own.at[5]),
    ]
    for c in here:
        c.start()
    g_across.forward()
    g_across.wait_recv()
    g_along.wait_recv()
    p_along.wait_recv()
    for c in here:
        c.wait()
    for c in (across, along, g_across, g_along, p_along):
        c.wait_send()


class Spread:
    def __init__(self, rows, cols, whole, first, second, done, sems):
        share = whole.shape[0] // rows.size
        mine = lambda p: pl.ds(pl.multiple_of(p * share, 8), share)
        one, two, three = sems
        self.rows, self.cols, self.mine = rows, cols, mine
        self.whole, self.first, self.second, self.done = whole, first, second, done
        self.one = Exchange(rows, lambda p: whole.at[mine(p)], lambda s: first.at[s], one)
        self.two = Exchange(cols, lambda p: second.at[cols.me], lambda s: second.at[s], two)
        self.three = Exchange(
            rows, lambda p: done.at[mine(rows.me)], lambda s: done.at[mine(s)], three
        )

    def start(self):
        self.first[self.rows.me] = self.whole[self.mine(self.rows.me), :]
        self.one.start()

    def turn(self):
        self.one.wait_recv()
        self.second[self.cols.me] = sum_slots(self.first, self.rows.size)
        self.two.start()

    def back(self):
        self.two.wait_recv()
        self.done[self.mine(self.rows.me), :] = sum_slots(self.second, self.cols.size)
        self.three.start()

    def finish(self):
        self.three.wait_recv()
        for e in (self.one, self.two, self.three):
            e.wait_send()


def last_kernel(
    n_row, n_col, node_count, ortho_ref, residual_ref, p_ref, image_x_ref, pr_ref, pc_ref,
    rr_ref, rc_ref, image_r_ref, early_ref, late_ref,
    first_in, second_in, second_out, inbox,
    e_whole, e_first, e_second, e_done, l_whole, l_first, l_second, l_done,
    s1, s2, s_row, e1, e2, e3, l1, l2, l3, own,
):
    rows, cols = Line("row", n_row), Line("col", n_col)
    plane = Plane(cols)
    k_width, mine = ortho_ref.shape
    blocks = mine // TILE
    enter(rows, cols)
    across = PlaneSum(plane, rr_ref, first_in, second_in, second_out, s1, s2, own)
    along = RowSum(rows, rc_ref, inbox, s_row, own.at[2])
    across.start()
    along.start()
    basis = jnp.concatenate([ortho_ref[...], residual_ref[...], p_ref[...]], axis=0)
    image_p = []
    for b in range(blocks):
        total = pr_ref[0, b].astype(F32)
        for j in range(1, n_col):
            total = total + pr_ref[j, b].astype(F32)
        for j in range(n_row):
            total = total + pc_ref[j, b].astype(F32)
        image_p.append(total)
    others = jnp.concatenate([image_x_ref[...], jnp.concatenate(image_p, axis=1)], axis=0)
    e_whole[:, : 2 * k_width] = dot_nt(basis, others) / node_count
    gram_b = dot_nt(basis, basis) / node_count
    pad = jnp.zeros((3 * k_width, k_width), F32)
    e_whole[:, 2 * k_width :] = jnp.concatenate([gram_b, pad], axis=1)
    early = Spread(rows, cols, e_whole, e_first, e_second, e_done, (e1, e2, e3))
    late = Spread(rows, cols, l_whole, l_first, l_second, l_done, (l1, l2, l3))
    early.start()
    across.pass_on(k_width)
    early.turn()
    from_rows = along.finish(blocks, k_width)
    images = add_lists([across.finish(k_width), from_rows])
    image_r = jnp.concatenate(images, axis=1)
    image_r_ref[...] = image_r
    l_whole[...] = jnp.concatenate([dot_nt(basis, image_r) / node_count, pad], axis=1)
    late.start()
    early.back()
    late.turn()
    late.back()
    early.finish()
    early_ref[...] = e_done[...]
    late.finish()
    late_ref[...] = l_done[...]
    across.wait_send()
    along.wait_send()


def hand_kernel(residual_in, image_in, early_ref, late_ref, residual_ref, image_ref, a_ref, b_ref):
    residual_ref[...] = residual_in[...]
    image_ref[...] = image_in[...]
    k_width = residual_in.shape[0]
    x_cols, p_cols = early_ref[:, :k_width], early_ref[:, k_width : 2 * k_width]
    a_ref[...] = jnp.concatenate([x_cols, late_ref[:, :k_width], p_cols], axis=1)
    b_ref[...] = early_ref[:, 2 * k_width : 5 * k_width]


def per_device(block_x, block_p, tile_rows, tile_cols, tile_count, tile_vals):
    n_row, n_col = lax.axis_size("row"), lax.axis_size("col")
    k_width, mine = block_x.shape
    node_count = mine * n_row * n_col
    blocks = mine // TILE
    slots = tile_vals.shape[2]
    vals = tile_vals.reshape(slots, TILE, TILE)
    vmem = pl.BlockSpec(memory_space=pltpu.VMEM)
    anywhere = pl.BlockSpec(memory_space=pl.ANY)
    row_sems = pltpu.SemaphoreType.DMA((2, n_row))
    col_sems = pltpu.SemaphoreType.DMA((2, n_col))
    plane_sems = pltpu.SemaphoreType.DMA((2, 2, SIDE, SIDE))
    ring_sems = pltpu.SemaphoreType.DMA((2, 2, SIDE))
    shape = jax.ShapeDtypeStruct
    params = lambda i: pltpu.CompilerParams(
        collective_id=i, has_side_effects=True, vmem_limit_bytes=VMEM_LIMIT
    )
    local = shape((k_width, mine), F32)
    half_rows, all_rows = HALF * k_width + SPARE, blocks * k_width + SPARE
    sum_boxes = [
        pltpu.VMEM((2, SIDE, SIDE, half_rows, TILE), jnp.int16),
        pltpu.VMEM((2, SIDE, half_rows, TILE), jnp.int16),
        pltpu.VMEM((2, SIDE, half_rows, TILE), jnp.int16),
        pltpu.VMEM((n_row, all_rows, TILE), jnp.int16),
    ]
    small = [
        pltpu.VMEM((n_row, k_width // 2, 2 * k_width), F32),
        pltpu.VMEM((n_col, k_width // 2, 2 * k_width), F32),
    ]

    ortho, vrow, vcol = pl.pallas_call(
        functools.partial(first_kernel, n_row, n_col, node_count),
        in_specs=[vmem] * 2,
        out_specs=[vmem, anywhere, anywhere],
        out_shape=[
            local,
            shape((n_col, blocks, 2 * k_width, TILE), BF16),
            shape((n_row, blocks, 2 * k_width, TILE), BF16),
        ],
        scratch_shapes=[
            pltpu.VMEM((blocks, 2 * k_width, TILE), BF16),
            *small,
            row_sems, col_sems, row_sems, plane_sems, row_sems, plane_sems,
            pltpu.SemaphoreType.DMA((2,)),
        ],
        compiler_params=params(0),
    )(block_x, block_p)

    xr, xc, pr, pc = apply_graph(tile_rows, tile_cols, tile_count, vrow, vcol, vals, k_width)
    pc = pc.reshape(n_row, blocks, k_width, TILE)

    residual, image_x, vrow, vcol, pc = pl.pallas_call(
        functools.partial(middle_kernel, n_row, n_col, node_count),
        in_specs=[vmem] + [anywhere] * 3,
        out_specs=[vmem, vmem] + [anywhere] * 3,
        out_shape=[
            local, local,
            shape((n_col, blocks, k_width, TILE), BF16),
            shape((n_row, blocks, k_width, TILE), BF16),
            shape((n_row, blocks, k_width, TILE), BF16),
        ],
        scratch_shapes=[
            *sum_boxes,
            pltpu.VMEM((blocks, k_width, TILE), BF16),
            *small,
            plane_sems, ring_sems, row_sems, row_sems, col_sems, row_sems, plane_sems, row_sems,
            pltpu.SemaphoreType.DMA((6,)),
        ],
        compiler_params=params(1),
    )(ortho, xr, xc, pc)

    pr, vcol = lax.optimization_barrier((pr, vcol))
    pr = lax.all_to_all(
        pr.reshape(n_col, blocks, k_width, TILE), "col", split_axis=0, concat_axis=0, tiled=True
    )

    rr, rc = apply_graph(tile_rows, tile_cols, tile_count, vrow, vcol, vals, k_width)

    full = 3 * k_width
    spread = lambda width: [
        pltpu.VMEM((full, width), F32),
        pltpu.VMEM((n_row, full // n_row, width), F32),
        pltpu.VMEM((n_col, full // n_row, width), F32),
        pltpu.VMEM((full, width), F32),
    ]
    image_r, early, late = pl.pallas_call(
        functools.partial(last_kernel, n_row, n_col, node_count),
        in_specs=[vmem] * 6 + [anywhere] * 2,
        out_specs=[vmem] * 3,
        out_shape=[local, shape((full, 6 * k_width), F32), shape((full, 2 * k_width), F32)],
        scratch_shapes=[
            *sum_boxes, *spread(6 * k_width), *spread(2 * k_width),
            plane_sems, ring_sems, row_sems,
            row_sems, col_sems, row_sems, row_sems, col_sems, row_sems,
            pltpu.SemaphoreType.DMA((3,)),
        ],
        compiler_params=params(2),
    )(ortho, residual, block_p, image_x, pr, pc, rr, rc)
    return tuple(
        pl.pallas_call(
            hand_kernel,
            in_specs=[vmem] * 4,
            out_specs=[vmem] * 4,
            out_shape=[local, local, shape((full, full), F32), shape((full, full), F32)],
        )(residual, image_r, early, late)
    )


def solution(mesh):
    in_specs = (
        P(None, ("row", "col")),
        P(None, ("row", "col")),
        P("row", "col", None),
        P("row", "col", None),
        P("row", "col"),
        P("row", "col", None, None, None),
    )
    out_specs = (P(None, ("row", "col")), P(None, ("row", "col")), P(), P())
    return jax.shard_map(
        per_device, mesh=mesh, in_specs=in_specs, out_specs=out_specs, check_vma=False
    )
```

```python
import functools

import jax
import jax.numpy as jnp
from jax import lax
from jax.experimental import pallas as pl
from jax.experimental.pallas import tpu as pltpu
from jax.sharding import PartitionSpec as P

F32 = jnp.float32
BF16 = jnp.bfloat16
TILE = 128
HIGHEST = lax.Precision.HIGHEST
MESH = pl.DeviceIdType.MESH
VMEM_LIMIT = 56 * 2**20
GROUP = 48
SIDE = 4
HALF = 3
SPARE = 16
TOP = 32700.0


def dot_nt(left, right):
    return lax.dot_general(
        left, right, (((1,), (1,)), ((), ())), precision=HIGHEST, preferred_element_type=F32
    )


def dot_tn(left, right):
    return lax.dot_general(
        left, right, (((0,), (0,)), ((), ())), precision=HIGHEST, preferred_element_type=F32
    )


def dot_nn(left, right):
    return lax.dot_general(
        left, right, (((1,), (0,)), ((), ())), precision=HIGHEST, preferred_element_type=F32
    )


class Line:
    def __init__(self, name, size):
        self.name, self.size = name, size
        self.me = lax.axis_index(name)

    def ahead(self, k):
        return lax.rem(self.me + k, self.size)

    def behind(self, k):
        return lax.rem(self.me + self.size - k, self.size)

    def greet(self, barrier):
        for k in range(1, self.size):
            pl.semaphore_signal(
                barrier, inc=1, device_id={self.name: self.ahead(k)}, device_id_type=MESH
            )

    def copies(self, source, target, send_sem, recv_sem):
        return [
            pltpu.make_async_remote_copy(
                src_ref=source(self.ahead(k)),
                dst_ref=target(self.me),
                send_sem=send_sem.at[k],
                recv_sem=recv_sem.at[k],
                device_id={self.name: self.ahead(k)},
                device_id_type=MESH,
            )
            for k in range(1, self.size)
        ]

    def arrivals(self, source, target, send_sem, recv_sem):
        return [
            pltpu.make_async_remote_copy(
                src_ref=source(self.ahead(k)),
                dst_ref=target(self.behind(k)),
                send_sem=send_sem.at[k],
                recv_sem=recv_sem.at[k],
                device_id={self.name: self.ahead(k)},
                device_id_type=MESH,
            )
            for k in range(1, self.size)
        ]


class Exchange:
    def __init__(self, line, source, target, sems):
        self.sent = line.copies(source, target, sems.at[0], sems.at[1])
        self.come = line.arrivals(source, target, sems.at[0], sems.at[1])

    def start(self):
        for c in self.sent:
            c.start()
        return self

    def wait_recv(self):
        for c in self.come:
            c.wait_recv()
        return self

    def wait_send(self):
        for c in self.sent:
            c.wait_send()
        return self


def pack(parts, ref):
    width = parts[0].shape[0]
    if ref.dtype == BF16:
        for i, part in enumerate(parts):
            ref[i * width : (i + 1) * width, :] = part.astype(BF16)
        return
    most = jnp.abs(parts[0])
    for part in parts[1:]:
        most = jnp.maximum(most, jnp.abs(part))
    most = jnp.maximum(jnp.max(most, axis=1, keepdims=True), 1e-30)
    power = jnp.clip(jnp.ceil(jnp.log2(most)), -100.0, 126.0)
    up = jnp.exp2(-power) * TOP
    for i, part in enumerate(parts):
        ref[i * width : (i + 1) * width, :] = jnp.round(part * up).astype(jnp.int32).astype(jnp.int16)
    down = lax.broadcasted_iota(jnp.int32, (width, TILE), 0)
    across = lax.broadcasted_iota(jnp.int32, (width, TILE), 1)
    line = jnp.sum(jnp.where(down == across, power, 0.0), axis=0, keepdims=True)
    line = jnp.broadcast_to(line, (SPARE, TILE))
    ref[len(parts) * width :, :] = line.astype(jnp.int32).astype(jnp.int16)


def unpack(ref, count, width):
    if ref.dtype == BF16:
        return [ref[i * width : (i + 1) * width, :].astype(F32) for i in range(count)]
    line = ref[count * width :, :].astype(jnp.int32).astype(F32)[:1]
    down = lax.broadcasted_iota(jnp.int32, (width, TILE), 0)
    across = lax.broadcasted_iota(jnp.int32, (width, TILE), 1)
    power = jnp.sum(jnp.where(down == across, line, 0.0), axis=1, keepdims=True)
    step = jnp.exp2(power) * (1.0 / TOP)
    return [
        ref[i * width : (i + 1) * width, :].astype(jnp.int32).astype(F32) * step
        for i in range(count)
    ]


def add_lists(lists):
    return [functools.reduce(lambda a, b: a + b, parts) for parts in zip(*lists)]


class Plane:
    def __init__(self, cols):
        self.spot = (cols.me // SIDE, lax.rem(cols.me, SIDE))

    def axes(self, half):
        return (self.spot[0], self.spot[1]) if half == 0 else (self.spot[1], self.spot[0])

    def index(self, half, first, second):
        first, second = lax.rem(first, SIDE), lax.rem(second, SIDE)
        return first * SIDE + second if half == 0 else second * SIDE + first

    def copy(self, source, target, sems, at, device):
        return pltpu.make_async_remote_copy(
            src_ref=source,
            dst_ref=target,
            send_sem=sems.at[(0, *at)],
            recv_sem=sems.at[(1, *at)],
            device_id={"col": device},
            device_id_type=MESH,
        )


class PlaneGather:
    def __init__(self, plane, mine, slot, sems):
        self.plane, self.mine, self.slot, self.sems = plane, mine, slot, sems
        self.sent = []

    def send(self, source, owner, half, at, device):
        c = self.plane.copy(source, self.slot(owner, half), self.sems, at, device)
        c.start()
        self.sent.append(c)

    def arrived(self, owner, half, at):
        _, device = self.place(half, 1, 0)
        self.plane.copy(self.mine(half), self.slot(owner, half), self.sems, at, device).wait_recv()

    def place(self, half, first, second):
        f, s = self.plane.axes(half)
        return (
            self.plane.index(half, f + SIDE - first, s + SIDE - second),
            self.plane.index(half, f + first, s + second),
        )

    def start(self):
        for half in (0, 1):
            me, _ = self.place(half, 0, 0)
            for k in range(1, SIDE):
                self.send(self.mine(half), me, half, (half, k, 0), self.place(half, k, 0)[1])
        for half in (0, 1):
            me, _ = self.place(half, 0, 0)
            for k in range(1, SIDE):
                self.send(self.mine(half), me, half, (half, 0, k), self.place(half, 0, k)[1])

    def forward(self):
        for i in (1, 3, 2):
            for half in (0, 1):
                owner, _ = self.place(half, i, 0)
                self.arrived(owner, half, (half, i, 0))
                for k in range(1, SIDE):
                    self.send(
                        self.slot(owner, half), owner, half, (half, i, k), self.place(half, 0, k)[1]
                    )

    def wait_recv(self):
        for i in range(SIDE):
            for k in range(1, SIDE):
                for half in (0, 1):
                    self.arrived(self.place(half, i, k)[0], half, (half, i, k))

    def wait_send(self):
        for c in self.sent:
            c.wait_send()


class PlaneSum:
    def __init__(self, plane, packed, first_in, second_in, second_out, sems1, sems2, own):
        self.plane, self.packed = plane, packed
        self.first_in, self.second_in, self.second_out = first_in, second_in, second_out
        self.sems1, self.sems2 = sems1, sems2
        self.own = [
            pltpu.make_async_copy(
                packed.at[h, pl.ds(plane.axes(h)[0] * SIDE, SIDE)], first_in.at[h, 0], own.at[h]
            )
            for h in (0, 1)
        ]
        self.sent = []

    def hop(self, half, k, j):
        f, s = self.plane.axes(half)
        return self.plane.copy(
            self.packed.at[half, lax.rem(f + k, SIDE) * SIDE + j],
            self.first_in.at[half, k, j],
            self.sems1,
            (half, k, j),
            self.plane.index(half, f + k, s),
        )

    def hop2(self, half, k):
        f, s = self.plane.axes(half)
        return self.plane.copy(
            self.second_out.at[half, k],
            self.second_in.at[half, k],
            self.sems2,
            (half, k),
            self.plane.index(half, f, s + k),
        )

    def start(self):
        for n in (2, 1, 3, 0):
            for half in (0, 1):
                for k in (2, 1, 3):
                    c = self.hop(half, k, self.turn(half, n))
                    c.start()
                    self.sent.append(c)
        for c in self.own:
            c.start()

    def turn(self, half, n):
        return lax.rem(self.plane.axes(half)[1] + n, SIDE)

    def gathered(self, half, k, width):
        j = self.turn(half, k)
        for i in range(1, SIDE):
            self.hop(half, i, j).wait_recv()
        return add_lists(
            [unpack(self.first_in.at[half, i, j], HALF, width) for i in range(SIDE)]
        )

    def pass_on(self, width):
        for c in self.own:
            c.wait()
        for k in (2, 1, 3):
            for half in (0, 1):
                pack(self.gathered(half, k, width), self.second_out.at[half, k])
                c = self.hop2(half, k)
                c.start()
                self.sent.append(c)

    def finish(self, width):
        mine = [self.gathered(half, 0, width) for half in (0, 1)]
        blocks = []
        for half in (0, 1):
            parts = [mine[half]]
            for k in (2, 1, 3):
                self.hop2(half, k).wait_recv()
                parts.append(unpack(self.second_in.at[half, k], HALF, width))
            blocks += add_lists(parts)
        return blocks

    def wait_send(self):
        for c in self.sent:
            c.wait_send()


class RowSum:
    def __init__(self, rows, packed, inbox, sems, own):
        self.rows, self.inbox = rows, inbox
        self.move = Exchange(rows, lambda p: packed.at[p], lambda s: inbox.at[s], sems)
        self.own = pltpu.make_async_copy(packed.at[rows.me], inbox.at[rows.me], own)

    def start(self):
        self.move.start()
        self.own.start()

    def finish(self, count, width):
        self.own.wait()
        self.move.wait_recv()
        return add_lists([unpack(self.inbox.at[j], count, width) for j in range(self.rows.size)])

    def wait_send(self):
        self.move.wait_send()


def greet(rows, cols):
    barrier = pltpu.get_barrier_semaphore()
    rows.greet(barrier)
    cols.greet(barrier)


def meet(rows, cols):
    pl.semaphore_wait(pltpu.get_barrier_semaphore(), rows.size + cols.size - 2)


def sum_slots(ref, count):
    total = ref[0]
    for j in range(1, count):
        total = total + ref[j]
    return total


def all_reduce(rows, cols, part, first, second, row_sems, col_sems, between=None):
    half = part.shape[0] // 2
    first[rows.me] = jnp.concatenate([part[:half], part[half:]], axis=1)
    one = Exchange(rows, lambda p: first.at[rows.me], lambda s: first.at[s], row_sems)
    one.start().wait_recv()
    second[cols.me] = sum_slots(first, rows.size)
    two = Exchange(cols, lambda p: second.at[cols.me], lambda s: second.at[s], col_sems)
    two.start()
    if between is not None:
        between()
    two.wait_recv()
    total = sum_slots(second, cols.size)
    one.wait_send()
    two.wait_send()
    return jnp.concatenate([total[:, : 2 * half], total[:, 2 * half :]], axis=0)


def factor(gram):
    k_width = gram.shape[0]
    row_id = lax.broadcasted_iota(jnp.int32, (k_width, k_width), 0)
    col_id = lax.broadcasted_iota(jnp.int32, (k_width, k_width), 1)
    eye = jnp.where(row_id == col_id, 1.0, 0.0).astype(F32)
    work = jnp.concatenate([gram, eye], axis=1)
    down = lax.broadcasted_iota(jnp.int32, (k_width, 2 * k_width), 0)
    pivots = []
    for k in range(k_width):
        pivot_row = work[k : k + 1, :]
        pivot = work[k : k + 1, k : k + 1]
        pivots.append(pivot)
        if k + 1 < k_width:
            ratio = work[:, k : k + 1]
            work = work - jnp.where(down > k, ratio * (pivot_row * (1.0 / pivot)), 0.0)
    scale = lax.rsqrt(jnp.concatenate(pivots, axis=0))
    return work[:, k_width:] * scale


def first_kernel(
    n_row, n_col, node_count, x_ref, p_ref, ortho_ref, vrow_ref, vcol_ref,
    low, x, p, first, second, ar_row, ar_col, p_row, p_plane, x_row, x_plane, own, loads,
):
    rows, cols = Line("row", n_row), Line("col", n_col)
    plane = Plane(cols)
    k_width, mine = x_ref.shape
    blocks = mine // TILE
    fetched = [
        pltpu.make_async_copy(ref, to, loads.at[i]) for i, (ref, to) in enumerate(((x_ref, x), (p_ref, p)))
    ]
    for c in fetched:
        c.start()
    greet(rows, cols)
    fetched[0].wait()
    part = dot_nt(x[...], x[...]) / node_count
    fetched[1].wait()
    for b in range(blocks):
        low[b, k_width:, :] = p[:, b * TILE : (b + 1) * TILE].astype(BF16)
    meet(rows, cols)

    def gathers(band, row_sems, plane_sems):
        across = PlaneGather(
            plane,
            lambda h: low.at[pl.ds(h * HALF, HALF), band, :],
            lambda owner, h: vrow_ref.at[owner, pl.ds(h * HALF, HALF), band, :],
            plane_sems,
        )
        along = Exchange(
            rows, lambda p: low.at[:, band, :], lambda s: vcol_ref.at[s, :, band, :], row_sems
        )
        return across, along

    p_across, p_along = gathers(pl.ds(k_width, k_width), p_row, p_plane)
    x_across, x_along = gathers(pl.ds(0, k_width), x_row, x_plane)

    def give_p():
        p_across.start()
        p_along.start()

    gram = all_reduce(rows, cols, part, first, second, ar_row, ar_col, give_p)
    p_across.forward()
    ortho = dot_nn(factor(gram), x[...])
    ortho_ref[...] = ortho
    for b in range(blocks):
        low[b, :k_width, :] = ortho[:, b * TILE : (b + 1) * TILE].astype(BF16)
    x_across.start()
    x_along.start()
    here = [
        pltpu.make_async_copy(low, vrow_ref.at[cols.me], own.at[0]),
        pltpu.make_async_copy(low, vcol_ref.at[rows.me], own.at[1]),
    ]
    for c in here:
        c.start()
    x_across.forward()
    moves = (p_across, p_along, x_across, x_along)
    for m in moves:
        m.wait_recv()
    for m in moves:
        m.wait_send()
    for c in here:
        c.wait()


def times(left, right, right_dim):
    return lax.dot_general(
        left, right, (((1,), (right_dim,)), ((), ())), preferred_element_type=F32
    )


def apply_kernel(
    k_width, rows_ref, cols_ref, count_ref, vrow_ref, vcol_ref, tile_ref, *rest
):
    n_out = (len(rest) - 8) // 2
    outs, boxes = rest[:n_out], rest[n_out : 2 * n_out]
    vrow, vcol, tiles, row_acc, col_acc, tile_sems, in_sems, out_sems = rest[2 * n_out :]
    row_blocks, width, _ = vrow.shape
    col_blocks = vcol.shape[0]
    count = count_ref[0, 0]
    groups = (count + GROUP - 1) // GROUP

    def tile_copy(g):
        part = pl.ds(g * GROUP, GROUP)
        return pltpu.make_async_copy(tile_ref.at[part], tiles.at[part], tile_sems.at[g])

    def start_copy(g, carry):
        tile_copy(g).start()
        return carry

    inputs = [
        pltpu.make_async_copy(vcol_ref, vcol, in_sems.at[0]),
        pltpu.make_async_copy(vrow_ref, vrow, in_sems.at[1]),
    ]
    tile_copy(0).start()
    for c in inputs:
        c.start()
    lax.fori_loop(1, groups, start_copy, 0)
    row_acc[...] = jnp.zeros_like(row_acc)
    col_acc[...] = jnp.zeros_like(col_acc)
    for c in inputs:
        c.wait()

    def place(slot):
        live = slot < count
        a, b = rows_ref[0, 0, slot], cols_ref[0, 0, slot]
        return a, b, jnp.where(live, a, row_blocks), jnp.where(live, b, col_blocks)

    def single(slot):
        a, b, to_row, to_col = place(slot)
        tile = tiles[slot]
        row_acc[to_row] += times(vcol[b], tile, 1)
        col_acc[to_col] += times(vrow[a], tile, 0)

    def pair(slot):
        a, b, to_row, to_col = place(slot)
        a2, b2, to_row2, to_col2 = place(slot + 1)
        tile, tile2 = tiles[slot], tiles[slot + 1]
        none = jnp.zeros((width, TILE), BF16)

        def beside(u, v):
            return jnp.concatenate(
                [jnp.concatenate([u, none], axis=1), jnp.concatenate([none, v], axis=1)], axis=0
            )

        forward = times(beside(vcol[b], vcol[b2]), jnp.concatenate([tile, tile2], axis=1), 1)
        row_acc[to_row] += forward[:width]
        row_acc[to_row2] += forward[width:]
        backward = times(beside(vrow[a], vrow[a2]), jnp.concatenate([tile, tile2], axis=0), 0)
        col_acc[to_col] += backward[:width]
        col_acc[to_col2] += backward[width:]

    def group(g, carry):
        tile_copy(g).wait()
        if width < TILE:
            for u in range(0, GROUP, 2):
                pair(g * GROUP + u)
        else:
            for u in range(GROUP):
                single(g * GROUP + u)
        return carry

    lax.fori_loop(0, groups, group, 0)

    n_row, n_col = boxes[1].shape[0], boxes[0].shape[1]
    blocks = row_blocks // n_col
    results = [
        pltpu.make_async_copy(box, out, out_sems.at[i]) for i, (box, out) in enumerate(zip(boxes, outs))
    ]
    for i in range(n_out - 2, -1, -2):
        band = pl.ds(i // 2 * k_width, k_width)

        def pack_row(c, carry):
            for half in (0, 1):
                at = c if half == 0 else lax.rem(c, SIDE) * SIDE + c // SIDE
                parts = [row_acc[c * blocks + half * HALF + n, band, :] for n in range(HALF)]
                pack(parts, boxes[i].at[half, at])
            return carry

        def pack_col(r, carry):
            pack([col_acc[r * blocks + n, band, :] for n in range(blocks)], boxes[i + 1].at[r])
            return carry

        lax.fori_loop(0, n_col, pack_row, 0)
        results[i].start()
        lax.fori_loop(0, n_row, pack_col, 0)
        results[i + 1].start()
    for c in results:
        c.wait()


def apply_graph(tile_rows, tile_cols, count, vrow, vcol, vals, k_width):
    n_col, blocks, width, _ = vrow.shape
    n_row = vcol.shape[0]
    slots = vals.shape[0]
    row_blocks, col_blocks = n_col * blocks, n_row * blocks
    smem = pl.BlockSpec(memory_space=pltpu.SMEM)
    anywhere = pl.BlockSpec(memory_space=pl.ANY)
    shape = jax.ShapeDtypeStruct
    out_shape = [
        shape((2, n_col, HALF * k_width + SPARE, TILE), jnp.int16),
        shape((n_row, blocks * k_width + SPARE, TILE), jnp.int16),
    ]
    if width > k_width:
        out_shape += [
            shape((2, n_col, HALF * k_width, TILE), BF16),
            shape((n_row, blocks * k_width, TILE), BF16),
        ]
    return pl.pallas_call(
        functools.partial(apply_kernel, k_width),
        in_specs=[smem] * 3 + [anywhere] * 3,
        out_specs=[anywhere] * len(out_shape),
        out_shape=out_shape,
        scratch_shapes=[
            *[pltpu.VMEM(o.shape, o.dtype) for o in out_shape],
            pltpu.VMEM((row_blocks, width, TILE), BF16),
            pltpu.VMEM((col_blocks, width, TILE), BF16),
            pltpu.VMEM((slots, TILE, TILE), BF16),
            pltpu.VMEM((row_blocks + 1, width, TILE), F32),
            pltpu.VMEM((col_blocks + 1, width, TILE), F32),
            pltpu.SemaphoreType.DMA((slots // GROUP,)),
            pltpu.SemaphoreType.DMA((2,)),
            pltpu.SemaphoreType.DMA((len(out_shape),)),
        ],
        compiler_params=pltpu.CompilerParams(vmem_limit_bytes=VMEM_LIMIT),
        cost_estimate=pl.CostEstimate(
            flops=16 * slots * width * TILE * TILE,
            bytes_accessed=2 * slots * TILE * TILE,
            transcendentals=0,
        ),
    )(
        tile_rows, tile_cols, count,
        vrow.reshape(row_blocks, width, TILE), vcol.reshape(col_blocks, width, TILE), vals,
    )


def middle_kernel(
    n_row, n_col, node_count, ortho_ref, xr_ref, xc_ref, pr_ref, pc_ref,
    residual_ref, image_x_ref, image_p_ref, vrow_ref, vcol_ref,
    first_in, second_in, second_out, inbox, p_first_in, p_second_in, p_second_out, p_inbox,
    ortho, low, first, second,
    s1, s2, s_row, p1, p2, p_row, ar_row, ar_col, g_row, g_plane, own, loads,
):
    rows, cols = Line("row", n_row), Line("col", n_col)
    plane = Plane(cols)
    k_width, mine = ortho_ref.shape
    blocks = mine // TILE
    fetched = pltpu.make_async_copy(ortho_ref, ortho, loads.at[0])
    fetched.start()
    greet(rows, cols)
    meet(rows, cols)
    across = PlaneSum(plane, xr_ref, first_in, second_in, second_out, s1, s2, own)
    along = RowSum(rows, xc_ref, inbox, s_row, own.at[2])
    p_across = PlaneSum(plane, pr_ref, p_first_in, p_second_in, p_second_out, p1, p2, loads.at[pl.ds(1, 2)])
    p_along = RowSum(rows, pc_ref, p_inbox, p_row, loads.at[3])
    across.start()
    along.start()
    across.pass_on(k_width)
    p_across.start()
    from_rows = along.finish(blocks, k_width)
    images = add_lists([across.finish(k_width), from_rows])
    image_x_ref[...] = jnp.concatenate(images, axis=1)
    fetched.wait()
    part = dot_nt(ortho[...], image_x_ref[...]) / node_count

    def meanwhile():
        p_across.pass_on(k_width)
        p_along.start()

    rayleigh = all_reduce(rows, cols, part, first, second, ar_row, ar_col, meanwhile)
    residual = image_x_ref[...] - dot_tn(rayleigh, ortho[...])
    residual_ref[...] = residual
    for b in range(blocks):
        low[b] = residual[:, b * TILE : (b + 1) * TILE].astype(BF16)
    g_across = PlaneGather(
        plane,
        lambda h: low.at[pl.ds(h * HALF, HALF)],
        lambda owner, h: vrow_ref.at[owner, pl.ds(h * HALF, HALF)],
        g_plane,
    )
    g_along = Exchange(rows, lambda p: low, lambda s: vcol_ref.at[s], g_row)
    g_across.start()
    g_along.start()
    here = [
        pltpu.make_async_copy(low, vrow_ref.at[cols.me], own.at[3]),
        pltpu.make_async_copy(low, vcol_ref.at[rows.me], own.at[4]),
    ]
    for c in here:
        c.start()
    g_across.forward()
    p_images = add_lists([p_across.finish(k_width), p_along.finish(blocks, k_width)])
    image_p_ref[...] = jnp.concatenate(p_images, axis=1)
    g_across.wait_recv()
    g_along.wait_recv()
    for c in here:
        c.wait()
    for c in (across, along, p_across, p_along, g_across, g_along):
        c.wait_send()


class Spread:
    def __init__(self, rows, cols, whole, first, second, done, sems):
        share = whole.shape[0] // rows.size
        mine = lambda p: pl.ds(pl.multiple_of(p * share, 8), share)
        one, two, three = sems
        self.rows, self.cols, self.mine = rows, cols, mine
        self.whole, self.first, self.second, self.done = whole, first, second, done
        self.one = Exchange(rows, lambda p: whole.at[mine(p)], lambda s: first.at[s], one)
        self.two = Exchange(cols, lambda p: second.at[cols.me], lambda s: second.at[s], two)
        self.three = Exchange(
            rows, lambda p: done.at[mine(rows.me)], lambda s: done.at[mine(s)], three
        )

    def start(self):
        self.first[self.rows.me] = self.whole[self.mine(self.rows.me), :]
        self.one.start()

    def turn(self):
        self.one.wait_recv()
        self.second[self.cols.me] = sum_slots(self.first, self.rows.size)
        self.two.start()

    def back(self):
        self.two.wait_recv()
        self.done[self.mine(self.rows.me), :] = sum_slots(self.second, self.cols.size)
        self.three.start()

    def finish(self):
        self.three.wait_recv()
        for e in (self.one, self.two, self.three):
            e.wait_send()


def last_kernel(
    n_row, n_col, node_count, ortho_ref, residual_ref, p_ref, image_x_ref, image_p_ref,
    rr_ref, rc_ref, image_r_ref, early_ref, late_ref,
    first_in, second_in, second_out, inbox, basis, image_x, image_p,
    e_whole, e_first, e_second, e_done, l_whole, l_first, l_second, l_done,
    s1, s2, s_row, e1, e2, e3, l1, l2, l3, own, loads,
):
    rows, cols = Line("row", n_row), Line("col", n_col)
    plane = Plane(cols)
    k_width, mine = ortho_ref.shape
    blocks = mine // TILE
    sources = [(r, basis.at[pl.ds(i * k_width, k_width)]) for i, r in enumerate((ortho_ref, residual_ref, p_ref))]
    sources += [(image_x_ref, image_x), (image_p_ref, image_p)]
    fetched = [pltpu.make_async_copy(r, to, loads.at[i]) for i, (r, to) in enumerate(sources)]
    for c in fetched:
        c.start()
    greet(rows, cols)
    meet(rows, cols)
    across = PlaneSum(plane, rr_ref, first_in, second_in, second_out, s1, s2, own)
    along = RowSum(rows, rc_ref, inbox, s_row, own.at[2])
    across.start()
    along.start()
    for c in fetched:
        c.wait()
    e_whole[:, : 3 * k_width] = dot_nt(basis[...], basis[...]) / node_count
    e_whole[:, 3 * k_width :] = dot_nt(basis[...], image_x[...]) / node_count
    early = Spread(rows, cols, e_whole, e_first, e_second, e_done, (e1, e2, e3))
    late = Spread(rows, cols, l_whole, l_first, l_second, l_done, (l1, l2, l3))
    early.start()
    from_p = dot_nt(basis[...], image_p[...]) / node_count
    across.pass_on(k_width)
    early.turn()
    from_rows = along.finish(blocks, k_width)
    images = add_lists([across.finish(k_width), from_rows])
    image_r = jnp.concatenate(images, axis=1)
    image_r_ref[...] = image_r
    from_r = dot_nt(basis[...], image_r) / node_count
    l_whole[...] = jnp.concatenate([from_r, from_p], axis=1)
    late.start()
    late.turn()
    early.back()
    late.back()
    early.finish()
    early_ref[...] = e_done[...]
    late.finish()
    late_ref[...] = l_done[...]
    across.wait_send()
    along.wait_send()


def hand_kernel(residual_in, image_in, early_ref, late_ref, residual_ref, image_ref, a_ref, b_ref):
    residual_ref[...] = residual_in[...]
    image_ref[...] = image_in[...]
    k_width = residual_in.shape[0]
    a_ref[...] = jnp.concatenate([early_ref[:, 3 * k_width :], late_ref[...]], axis=1)
    b_ref[...] = early_ref[:, : 3 * k_width]


def per_device(block_x, block_p, tile_rows, tile_cols, tile_count, tile_vals):
    n_row, n_col = lax.axis_size("row"), lax.axis_size("col")
    k_width, mine = block_x.shape
    node_count = mine * n_row * n_col
    blocks = mine // TILE
    slots = tile_vals.shape[2]
    vals = tile_vals.reshape(slots, TILE, TILE)
    vmem = pl.BlockSpec(memory_space=pltpu.VMEM)
    anywhere = pl.BlockSpec(memory_space=pl.ANY)
    row_sems = pltpu.SemaphoreType.DMA((2, n_row))
    col_sems = pltpu.SemaphoreType.DMA((2, n_col))
    plane_sems = pltpu.SemaphoreType.DMA((2, 2, SIDE, SIDE))
    ring_sems = pltpu.SemaphoreType.DMA((2, 2, SIDE))
    shape = jax.ShapeDtypeStruct
    params = lambda i: pltpu.CompilerParams(
        collective_id=i, has_side_effects=True, vmem_limit_bytes=VMEM_LIMIT
    )
    local = shape((k_width, mine), F32)
    half_rows, all_rows = HALF * k_width + SPARE, blocks * k_width + SPARE
    sum_boxes = [
        pltpu.VMEM((2, SIDE, SIDE, half_rows, TILE), jnp.int16),
        pltpu.VMEM((2, SIDE, half_rows, TILE), jnp.int16),
        pltpu.VMEM((2, SIDE, half_rows, TILE), jnp.int16),
        pltpu.VMEM((n_row, all_rows, TILE), jnp.int16),
    ]
    small = [
        pltpu.VMEM((n_row, k_width // 2, 2 * k_width), F32),
        pltpu.VMEM((n_col, k_width // 2, 2 * k_width), F32),
    ]

    ortho, vrow, vcol = pl.pallas_call(
        functools.partial(first_kernel, n_row, n_col, node_count),
        in_specs=[anywhere] * 2,
        out_specs=[vmem, anywhere, anywhere],
        out_shape=[
            local,
            shape((n_col, blocks, 2 * k_width, TILE), BF16),
            shape((n_row, blocks, 2 * k_width, TILE), BF16),
        ],
        scratch_shapes=[
            pltpu.VMEM((blocks, 2 * k_width, TILE), BF16),
            pltpu.VMEM((k_width, mine), F32),
            pltpu.VMEM((k_width, mine), F32),
            *small,
            row_sems, col_sems, row_sems, plane_sems, row_sems, plane_sems,
            pltpu.SemaphoreType.DMA((2,)),
            pltpu.SemaphoreType.DMA((2,)),
        ],
        compiler_params=params(0),
    )(block_x, block_p)

    xr, xc, pr, pc = apply_graph(tile_rows, tile_cols, tile_count, vrow, vcol, vals, k_width)

    residual, image_x, image_p, vrow, vcol = pl.pallas_call(
        functools.partial(middle_kernel, n_row, n_col, node_count),
        in_specs=[anywhere] * 5,
        out_specs=[vmem] * 3 + [anywhere] * 2,
        out_shape=[
            local, local, local,
            shape((n_col, blocks, k_width, TILE), BF16),
            shape((n_row, blocks, k_width, TILE), BF16),
        ],
        scratch_shapes=[
            *sum_boxes,
            pltpu.VMEM((2, SIDE, SIDE, HALF * k_width, TILE), BF16),
            pltpu.VMEM((2, SIDE, HALF * k_width, TILE), BF16),
            pltpu.VMEM((2, SIDE, HALF * k_width, TILE), BF16),
            pltpu.VMEM((n_row, blocks * k_width, TILE), BF16),
            pltpu.VMEM((k_width, mine), F32),
            pltpu.VMEM((blocks, k_width, TILE), BF16),
            *small,
            plane_sems, ring_sems, row_sems, plane_sems, ring_sems, row_sems,
            row_sems, col_sems, row_sems, plane_sems,
            pltpu.SemaphoreType.DMA((5,)),
            pltpu.SemaphoreType.DMA((4,)),
        ],
        compiler_params=params(1),
    )(ortho, xr, xc, pr, pc)

    rr, rc = apply_graph(tile_rows, tile_cols, tile_count, vrow, vcol, vals, k_width)

    full = 3 * k_width
    spread = lambda width: [
        pltpu.VMEM((full, width), F32),
        pltpu.VMEM((n_row, full // n_row, width), F32),
        pltpu.VMEM((n_col, full // n_row, width), F32),
        pltpu.VMEM((full, width), F32),
    ]
    image_r, early, late = pl.pallas_call(
        functools.partial(last_kernel, n_row, n_col, node_count),
        in_specs=[anywhere] * 7,
        out_specs=[vmem] * 3,
        out_shape=[local, shape((full, 4 * k_width), F32), shape((full, 2 * k_width), F32)],
        scratch_shapes=[
            *sum_boxes,
            pltpu.VMEM((full, mine), F32),
            pltpu.VMEM((k_width, mine), F32),
            pltpu.VMEM((k_width, mine), F32),
            *spread(4 * k_width), *spread(2 * k_width),
            plane_sems, ring_sems, row_sems,
            row_sems, col_sems, row_sems, row_sems, col_sems, row_sems,
            pltpu.SemaphoreType.DMA((3,)),
            pltpu.SemaphoreType.DMA((5,)),
        ],
        compiler_params=params(2),
    )(ortho, residual, block_p, image_x, image_p, rr, rc)
    return tuple(
        pl.pallas_call(
            hand_kernel,
            in_specs=[vmem] * 4,
            out_specs=[vmem] * 4,
            out_shape=[local, local, shape((full, full), F32), shape((full, full), F32)],
        )(residual, image_r, early, late)
    )


def solution(mesh):
    in_specs = (
        P(None, ("row", "col")),
        P(None, ("row", "col")),
        P("row", "col", None),
        P("row", "col", None),
        P("row", "col"),
        P("row", "col", None, None, None),
    )
    out_specs = (P(None, ("row", "col")), P(None, ("row", "col")), P(), P())
    return jax.shard_map(
        per_device, mesh=mesh, in_specs=in_specs, out_specs=out_specs, check_vma=False
    )
```

```python
import functools

import jax
import jax.numpy as jnp
from jax import lax
from jax.experimental import pallas as pl
from jax.experimental.pallas import tpu as pltpu
from jax.sharding import PartitionSpec as P

F32 = jnp.float32
BF16 = jnp.bfloat16
TILE = 128
HIGHEST = lax.Precision.HIGHEST
MESH = pl.DeviceIdType.MESH
GROUP = 48
SIDE = 4
HALF = 3
SPARE = 16
TOP = 32700.0


def dot_nt(left, right):
    return lax.dot_general(
        left, right, (((1,), (1,)), ((), ())), precision=HIGHEST, preferred_element_type=F32
    )


def dot_tn(left, right):
    return lax.dot_general(
        left, right, (((0,), (0,)), ((), ())), precision=HIGHEST, preferred_element_type=F32
    )


def dot_nn(left, right):
    return lax.dot_general(
        left, right, (((1,), (0,)), ((), ())), precision=HIGHEST, preferred_element_type=F32
    )


class Line:
    def __init__(self, name, size):
        self.name, self.size = name, size
        self.me = lax.axis_index(name)

    def ahead(self, k):
        return lax.rem(self.me + k, self.size)

    def behind(self, k):
        return lax.rem(self.me + self.size - k, self.size)

    def greet(self, barrier):
        for k in range(1, self.size):
            pl.semaphore_signal(
                barrier, inc=1, device_id={self.name: self.ahead(k)}, device_id_type=MESH
            )

    def copies(self, source, target, send_sem, recv_sem):
        return [
            pltpu.make_async_remote_copy(
                src_ref=source(self.ahead(k)),
                dst_ref=target(self.me),
                send_sem=send_sem.at[k],
                recv_sem=recv_sem.at[k],
                device_id={self.name: self.ahead(k)},
                device_id_type=MESH,
            )
            for k in range(1, self.size)
        ]

    def arrivals(self, source, target, send_sem, recv_sem):
        return [
            pltpu.make_async_remote_copy(
                src_ref=source(self.ahead(k)),
                dst_ref=target(self.behind(k)),
                send_sem=send_sem.at[k],
                recv_sem=recv_sem.at[k],
                device_id={self.name: self.ahead(k)},
                device_id_type=MESH,
            )
            for k in range(1, self.size)
        ]


class Exchange:
    def __init__(self, line, source, target, sems):
        self.sent = line.copies(source, target, sems.at[0], sems.at[1])
        self.come = line.arrivals(source, target, sems.at[0], sems.at[1])

    def start(self):
        for c in self.sent:
            c.start()
        return self

    def wait_recv(self):
        for c in self.come:
            c.wait_recv()
        return self

    def wait_send(self):
        for c in self.sent:
            c.wait_send()
        return self


def pack(parts, ref):
    width = parts[0].shape[0]
    if ref.dtype == BF16:
        for i, part in enumerate(parts):
            ref[i * width : (i + 1) * width, :] = part.astype(BF16)
        return
    most = jnp.abs(parts[0])
    for part in parts[1:]:
        most = jnp.maximum(most, jnp.abs(part))
    most = jnp.maximum(jnp.max(most, axis=1, keepdims=True), 1e-30)
    power = jnp.clip(jnp.ceil(jnp.log2(most)), -100.0, 126.0)
    up = jnp.exp2(-power) * TOP
    for i, part in enumerate(parts):
        ref[i * width : (i + 1) * width, :] = jnp.round(part * up).astype(jnp.int32).astype(jnp.int16)
    down = lax.broadcasted_iota(jnp.int32, (width, TILE), 0)
    across = lax.broadcasted_iota(jnp.int32, (width, TILE), 1)
    line = jnp.sum(jnp.where(down == across, power, 0.0), axis=0, keepdims=True)
    line = jnp.broadcast_to(line, (SPARE, TILE))
    ref[len(parts) * width :, :] = line.astype(jnp.int32).astype(jnp.int16)


def unpack(ref, count, width):
    if ref.dtype == BF16:
        return [ref[i * width : (i + 1) * width, :].astype(F32) for i in range(count)]
    line = ref[count * width :, :].astype(jnp.int32).astype(F32)[:1]
    down = lax.broadcasted_iota(jnp.int32, (width, TILE), 0)
    across = lax.broadcasted_iota(jnp.int32, (width, TILE), 1)
    power = jnp.sum(jnp.where(down == across, line, 0.0), axis=1, keepdims=True)
    step = jnp.exp2(power) * (1.0 / TOP)
    return [
        ref[i * width : (i + 1) * width, :].astype(jnp.int32).astype(F32) * step
        for i in range(count)
    ]


def add_lists(lists):
    return [functools.reduce(lambda a, b: a + b, parts) for parts in zip(*lists)]


class Plane:
    def __init__(self, cols):
        self.spot = (cols.me // SIDE, lax.rem(cols.me, SIDE))

    def axes(self, half):
        return (self.spot[0], self.spot[1]) if half == 0 else (self.spot[1], self.spot[0])

    def index(self, half, first, second):
        first, second = lax.rem(first, SIDE), lax.rem(second, SIDE)
        return first * SIDE + second if half == 0 else second * SIDE + first

    def copy(self, source, target, sems, at, device):
        return pltpu.make_async_remote_copy(
            src_ref=source,
            dst_ref=target,
            send_sem=sems.at[(0, *at)],
            recv_sem=sems.at[(1, *at)],
            device_id={"col": device},
            device_id_type=MESH,
        )


class PlaneGather:
    def __init__(self, plane, mine, slot, sems):
        self.plane, self.mine, self.slot, self.sems = plane, mine, slot, sems
        self.sent = []

    def send(self, source, owner, half, at, device):
        c = self.plane.copy(source, self.slot(owner, half), self.sems, at, device)
        c.start()
        self.sent.append(c)

    def arrived(self, owner, half, at):
        _, device = self.place(half, 1, 0)
        self.plane.copy(self.mine(half), self.slot(owner, half), self.sems, at, device).wait_recv()

    def place(self, half, first, second):
        f, s = self.plane.axes(half)
        return (
            self.plane.index(half, f + SIDE - first, s + SIDE - second),
            self.plane.index(half, f + first, s + second),
        )

    def start(self):
        for half in (0, 1):
            me, _ = self.place(half, 0, 0)
            for k in range(1, SIDE):
                self.send(self.mine(half), me, half, (half, k, 0), self.place(half, k, 0)[1])
        for half in (0, 1):
            me, _ = self.place(half, 0, 0)
            for k in range(1, SIDE):
                self.send(self.mine(half), me, half, (half, 0, k), self.place(half, 0, k)[1])

    def forward(self):
        for i in (1, 3, 2):
            for half in (0, 1):
                owner, _ = self.place(half, i, 0)
                self.arrived(owner, half, (half, i, 0))
                for k in range(1, SIDE):
                    self.send(
                        self.slot(owner, half), owner, half, (half, i, k), self.place(half, 0, k)[1]
                    )

    def wait_recv(self):
        for i in range(SIDE):
            for k in range(1, SIDE):
                for half in (0, 1):
                    self.arrived(self.place(half, i, k)[0], half, (half, i, k))

    def wait_send(self):
        for c in self.sent:
            c.wait_send()


class PlaneSum:
    def __init__(self, plane, packed, first_in, second_in, second_out, sems1, sems2, own):
        self.plane, self.packed = plane, packed
        self.first_in, self.second_in, self.second_out = first_in, second_in, second_out
        self.sems1, self.sems2 = sems1, sems2
        self.own = [
            pltpu.make_async_copy(
                packed.at[h, pl.ds(plane.axes(h)[0] * SIDE, SIDE)], first_in.at[h, 0], own.at[h]
            )
            for h in (0, 1)
        ]
        self.sent = []

    def hop(self, half, k, j):
        f, s = self.plane.axes(half)
        return self.plane.copy(
            self.packed.at[half, lax.rem(f + k, SIDE) * SIDE + j],
            self.first_in.at[half, k, j],
            self.sems1,
            (half, k, j),
            self.plane.index(half, f + k, s),
        )

    def hop2(self, half, k):
        f, s = self.plane.axes(half)
        return self.plane.copy(
            self.second_out.at[half, k],
            self.second_in.at[half, k],
            self.sems2,
            (half, k),
            self.plane.index(half, f, s + k),
        )

    def start(self):
        for n in (2, 1, 3, 0):
            for half in (0, 1):
                for k in (2, 1, 3):
                    c = self.hop(half, k, self.turn(half, n))
                    c.start()
                    self.sent.append(c)
        for c in self.own:
            c.start()

    def turn(self, half, n):
        return lax.rem(self.plane.axes(half)[1] + n, SIDE)

    def gathered(self, half, k, width):
        j = self.turn(half, k)
        for i in range(1, SIDE):
            self.hop(half, i, j).wait_recv()
        return add_lists(
            [unpack(self.first_in.at[half, i, j], HALF, width) for i in range(SIDE)]
        )

    def pass_on(self, width):
        for c in self.own:
            c.wait()
        for k in (2, 1, 3):
            for half in (0, 1):
                pack(self.gathered(half, k, width), self.second_out.at[half, k])
                c = self.hop2(half, k)
                c.start()
                self.sent.append(c)

    def finish(self, width):
        mine = [self.gathered(half, 0, width) for half in (0, 1)]
        blocks = []
        for half in (0, 1):
            parts = [mine[half]]
            for k in (2, 1, 3):
                self.hop2(half, k).wait_recv()
                parts.append(unpack(self.second_in.at[half, k], HALF, width))
            blocks += add_lists(parts)
        return blocks

    def wait_send(self):
        for c in self.sent:
            c.wait_send()


class RowSum:
    def __init__(self, rows, packed, inbox, sems, own):
        self.rows, self.inbox = rows, inbox
        self.move = Exchange(rows, lambda p: packed.at[p], lambda s: inbox.at[s], sems)
        self.own = pltpu.make_async_copy(packed.at[rows.me], inbox.at[rows.me], own)

    def start(self):
        self.move.start()
        self.own.start()

    def finish(self, count, width):
        self.own.wait()
        self.move.wait_recv()
        return add_lists([unpack(self.inbox.at[j], count, width) for j in range(self.rows.size)])

    def wait_send(self):
        self.move.wait_send()


def greet(rows, cols):
    barrier = pltpu.get_barrier_semaphore()
    rows.greet(barrier)
    cols.greet(barrier)


def meet(rows, cols):
    pl.semaphore_wait(pltpu.get_barrier_semaphore(), rows.size + cols.size - 2)


def sum_slots(ref, count):
    total = ref[0]
    for j in range(1, count):
        total = total + ref[j]
    return total


def all_reduce(
    rows, cols, part, first, second, row_sems, col_sems, between=None, before=None
):
    half = part.shape[0] // 2
    first[rows.me] = jnp.concatenate([part[:half], part[half:]], axis=1)
    one = Exchange(rows, lambda p: first.at[rows.me], lambda s: first.at[s], row_sems)
    one.start()
    if before is not None:
        before()
    one.wait_recv()
    second[cols.me] = sum_slots(first, rows.size)
    two = Exchange(cols, lambda p: second.at[cols.me], lambda s: second.at[s], col_sems)
    two.start()
    if between is not None:
        between()
    two.wait_recv()
    total = sum_slots(second, cols.size)
    one.wait_send()
    two.wait_send()
    return jnp.concatenate([total[:, : 2 * half], total[:, 2 * half :]], axis=0)


def factor(gram):
    k_width = gram.shape[0]
    row_id = lax.broadcasted_iota(jnp.int32, (k_width, k_width), 0)
    col_id = lax.broadcasted_iota(jnp.int32, (k_width, k_width), 1)
    eye = jnp.where(row_id == col_id, 1.0, 0.0).astype(F32)
    work = jnp.concatenate([gram, eye], axis=1)
    down = lax.broadcasted_iota(jnp.int32, (k_width, 2 * k_width), 0)
    pivots = []
    for k in range(k_width):
        pivot_row = work[k : k + 1, :]
        pivot = work[k : k + 1, k : k + 1]
        pivots.append(pivot)
        if k + 1 < k_width:
            ratio = work[:, k : k + 1]
            work = work - jnp.where(down > k, ratio * (pivot_row * (1.0 / pivot)), 0.0)
    scale = lax.rsqrt(jnp.concatenate(pivots, axis=0))
    return work[:, k_width:] * scale


def first_kernel(
    n_row, n_col, node_count, x_ref, p_ref, ortho_ref, vrow_ref, vcol_ref,
    low, x, p, first, second, ar_row, ar_col, p_row, p_plane, x_row, x_plane, own, loads,
):
    rows, cols = Line("row", n_row), Line("col", n_col)
    plane = Plane(cols)
    k_width, mine = x_ref.shape
    blocks = mine // TILE
    fetched = [
        pltpu.make_async_copy(ref, to, loads.at[i]) for i, (ref, to) in enumerate(((x_ref, x), (p_ref, p)))
    ]
    for c in fetched:
        c.start()
    greet(rows, cols)
    fetched[0].wait()
    part = dot_nt(x[...], x[...]) / node_count
    fetched[1].wait()
    for b in range(blocks):
        low[b, k_width:, :] = p[:, b * TILE : (b + 1) * TILE].astype(BF16)
    meet(rows, cols)

    def gathers(band, row_sems, plane_sems):
        across = PlaneGather(
            plane,
            lambda h: low.at[pl.ds(h * HALF, HALF), band, :],
            lambda owner, h: vrow_ref.at[owner, pl.ds(h * HALF, HALF), band, :],
            plane_sems,
        )
        along = Exchange(
            rows, lambda p: low.at[:, band, :], lambda s: vcol_ref.at[s, :, band, :], row_sems
        )
        return across, along

    p_across, p_along = gathers(pl.ds(k_width, k_width), p_row, p_plane)
    x_across, x_along = gathers(pl.ds(0, k_width), x_row, x_plane)

    def pass_p():
        p_across.forward()
        p_along.start()

    gram = all_reduce(
        rows, cols, part, first, second, ar_row, ar_col, pass_p, p_across.start
    )
    ortho = dot_nn(factor(gram), x[...])
    ortho_ref[...] = ortho
    for b in range(blocks):
        low[b, :k_width, :] = ortho[:, b * TILE : (b + 1) * TILE].astype(BF16)
    x_across.start()
    x_along.start()
    here = [
        pltpu.make_async_copy(low, vrow_ref.at[cols.me], own.at[0]),
        pltpu.make_async_copy(low, vcol_ref.at[rows.me], own.at[1]),
    ]
    for c in here:
        c.start()
    x_across.forward()
    moves = (p_across, p_along, x_across, x_along)
    for m in moves:
        m.wait_recv()
    for m in moves:
        m.wait_send()
    for c in here:
        c.wait()


def times(left, right, right_dim):
    return lax.dot_general(
        left, right, (((1,), (right_dim,)), ((), ())), preferred_element_type=F32
    )


def apply_kernel(
    k_width, rows_in, cols_in, count_ref, vrow_ref, vcol_ref, tile_ref, *rest
):
    n_out = (len(rest) - 10) // 2
    outs, boxes = rest[:n_out], rest[n_out : 2 * n_out]
    rows_ref, cols_ref, vrow, vcol, tiles, row_acc, col_acc, tile_sems, in_sems, out_sems = rest[2 * n_out :]
    row_blocks, width, _ = vrow.shape
    col_blocks = vcol.shape[0]
    count = count_ref[0, 0]
    groups = (count + GROUP - 1) // GROUP

    def tile_copy(g):
        part = pl.ds(g * GROUP, GROUP)
        return pltpu.make_async_copy(tile_ref.at[part], tiles.at[part], tile_sems.at[g])

    def start_copy(g, carry):
        tile_copy(g).start()
        return carry

    inputs = [
        pltpu.make_async_copy(vcol_ref, vcol, in_sems.at[0]),
        pltpu.make_async_copy(vrow_ref, vrow, in_sems.at[1]),
        pltpu.make_async_copy(rows_in, rows_ref, in_sems.at[2]),
        pltpu.make_async_copy(cols_in, cols_ref, in_sems.at[3]),
    ]
    for c in inputs:
        c.start()
    tile_copy(0).start()
    lax.fori_loop(1, groups, start_copy, 0)
    row_acc[...] = jnp.zeros_like(row_acc)
    col_acc[...] = jnp.zeros_like(col_acc)
    for c in inputs:
        c.wait()

    def place(slot):
        live = slot < count
        a, b = rows_ref[0, 0, slot], cols_ref[0, 0, slot]
        return a, b, jnp.where(live, a, row_blocks), jnp.where(live, b, col_blocks)

    def single(slot):
        a, b, to_row, to_col = place(slot)
        tile = tiles[slot]
        row_acc[to_row] += times(vcol[b], tile, 1)
        col_acc[to_col] += times(vrow[a], tile, 0)

    def pair(slot):
        a, b, to_row, to_col = place(slot)
        a2, b2, to_row2, to_col2 = place(slot + 1)
        tile, tile2 = tiles[slot], tiles[slot + 1]
        none = jnp.zeros((width, TILE), BF16)

        def beside(u, v):
            return jnp.concatenate(
                [jnp.concatenate([u, none], axis=1), jnp.concatenate([none, v], axis=1)], axis=0
            )

        forward = times(beside(vcol[b], vcol[b2]), jnp.concatenate([tile, tile2], axis=1), 1)
        row_acc[to_row] += forward[:width]
        row_acc[to_row2] += forward[width:]
        backward = times(beside(vrow[a], vrow[a2]), jnp.concatenate([tile, tile2], axis=0), 0)
        col_acc[to_col] += backward[:width]
        col_acc[to_col2] += backward[width:]

    def group(g, carry):
        tile_copy(g).wait()
        if width < TILE:
            for u in range(0, GROUP, 2):
                pair(g * GROUP + u)
        else:
            for u in range(GROUP):
                single(g * GROUP + u)
        return carry

    lax.fori_loop(0, groups, group, 0)

    n_row, n_col = boxes[1].shape[0], boxes[0].shape[1]
    blocks = row_blocks // n_col
    results = [
        pltpu.make_async_copy(box, out, out_sems.at[i]) for i, (box, out) in enumerate(zip(boxes, outs))
    ]
    for i in range(n_out - 2, -1, -2):
        band = pl.ds(i // 2 * k_width, k_width)

        def pack_row(c, carry):
            for half in (0, 1):
                at = c if half == 0 else lax.rem(c, SIDE) * SIDE + c // SIDE
                parts = [row_acc[c * blocks + half * HALF + n, band, :] for n in range(HALF)]
                pack(parts, boxes[i].at[half, at])
            return carry

        def pack_col(r, carry):
            pack([col_acc[r * blocks + n, band, :] for n in range(blocks)], boxes[i + 1].at[r])
            return carry

        lax.fori_loop(0, n_col, pack_row, 0)
        results[i].start()
        lax.fori_loop(0, n_row, pack_col, 0)
        results[i + 1].start()
    for c in results:
        c.wait()


def apply_graph(tile_rows, tile_cols, count, vrow, vcol, vals, k_width):
    n_col, blocks, width, _ = vrow.shape
    n_row = vcol.shape[0]
    slots = vals.shape[0]
    row_blocks, col_blocks = n_col * blocks, n_row * blocks
    smem = pl.BlockSpec(memory_space=pltpu.SMEM)
    in_hbm = pl.BlockSpec(memory_space=pltpu.HBM)
    anywhere = pl.BlockSpec(memory_space=pl.ANY)
    shape = jax.ShapeDtypeStruct
    out_shape = [
        shape((2, n_col, HALF * k_width + SPARE, TILE), jnp.int16),
        shape((n_row, blocks * k_width + SPARE, TILE), jnp.int16),
    ]
    if width > k_width:
        out_shape += [
            shape((2, n_col, HALF * k_width, TILE), BF16),
            shape((n_row, blocks * k_width, TILE), BF16),
        ]
    return pl.pallas_call(
        functools.partial(apply_kernel, k_width),
        in_specs=[in_hbm] * 2 + [smem] + [anywhere] * 2 + [in_hbm],
        out_specs=[anywhere] * len(out_shape),
        out_shape=out_shape,
        scratch_shapes=[
            *[pltpu.VMEM(o.shape, o.dtype) for o in out_shape],
            pltpu.SMEM(tile_rows.shape, jnp.int32),
            pltpu.SMEM(tile_cols.shape, jnp.int32),
            pltpu.VMEM((row_blocks, width, TILE), BF16),
            pltpu.VMEM((col_blocks, width, TILE), BF16),
            pltpu.VMEM((slots, TILE, TILE), BF16),
            pltpu.VMEM((row_blocks + 1, width, TILE), F32),
            pltpu.VMEM((col_blocks + 1, width, TILE), F32),
            pltpu.SemaphoreType.DMA((slots // GROUP,)),
            pltpu.SemaphoreType.DMA((4,)),
            pltpu.SemaphoreType.DMA((len(out_shape),)),
        ],
        compiler_params=pltpu.CompilerParams(vmem_limit_bytes=(24 + 18 * width // TILE) * 2**20),
        cost_estimate=pl.CostEstimate(
            flops=16 * slots * width * TILE * TILE,
            bytes_accessed=2 * slots * TILE * TILE,
            transcendentals=0,
        ),
    )(
        tile_rows, tile_cols, count,
        vrow.reshape(row_blocks, width, TILE), vcol.reshape(col_blocks, width, TILE), vals,
    )


def middle_kernel(
    n_row, n_col, node_count, ortho_ref, xr_ref, xc_ref, pr_ref, pc_ref,
    residual_ref, image_x_ref, image_p_ref, vrow_ref, vcol_ref,
    first_in, second_in, second_out, inbox, p_first_in, p_second_in, p_second_out, p_inbox,
    ortho, low, first, second,
    s1, s2, s_row, p1, p2, p_row, ar_row, ar_col, g_row, g_plane, own, loads,
):
    rows, cols = Line("row", n_row), Line("col", n_col)
    plane = Plane(cols)
    k_width, mine = ortho_ref.shape
    blocks = mine // TILE
    fetched = pltpu.make_async_copy(ortho_ref, ortho, loads.at[0])
    fetched.start()
    greet(rows, cols)
    meet(rows, cols)
    across = PlaneSum(plane, xr_ref, first_in, second_in, second_out, s1, s2, own)
    along = RowSum(rows, xc_ref, inbox, s_row, own.at[2])
    p_across = PlaneSum(plane, pr_ref, p_first_in, p_second_in, p_second_out, p1, p2, loads.at[pl.ds(1, 2)])
    p_along = RowSum(rows, pc_ref, p_inbox, p_row, loads.at[3])
    across.start()
    along.start()
    across.pass_on(k_width)
    p_across.start()
    from_rows = along.finish(blocks, k_width)
    images = add_lists([across.finish(k_width), from_rows])
    image_x_ref[...] = jnp.concatenate(images, axis=1)
    fetched.wait()
    part = dot_nt(ortho[...], image_x_ref[...]) / node_count

    def meanwhile():
        p_across.pass_on(k_width)
        p_along.start()

    rayleigh = all_reduce(rows, cols, part, first, second, ar_row, ar_col, meanwhile)
    residual = image_x_ref[...] - dot_tn(rayleigh, ortho[...])
    residual_ref[...] = residual
    for b in range(blocks):
        low[b] = residual[:, b * TILE : (b + 1) * TILE].astype(BF16)
    g_across = PlaneGather(
        plane,
        lambda h: low.at[pl.ds(h * HALF, HALF)],
        lambda owner, h: vrow_ref.at[owner, pl.ds(h * HALF, HALF)],
        g_plane,
    )
    g_along = Exchange(rows, lambda p: low, lambda s: vcol_ref.at[s], g_row)
    g_across.start()
    g_along.start()
    here = [
        pltpu.make_async_copy(low, vrow_ref.at[cols.me], own.at[3]),
        pltpu.make_async_copy(low, vcol_ref.at[rows.me], own.at[4]),
    ]
    for c in here:
        c.start()
    g_across.forward()
    p_images = add_lists([p_across.finish(k_width), p_along.finish(blocks, k_width)])
    image_p_ref[...] = jnp.concatenate(p_images, axis=1)
    g_across.wait_recv()
    g_along.wait_recv()
    for c in here:
        c.wait()
    for c in (across, along, p_across, p_along, g_across, g_along):
        c.wait_send()


class Spread:
    def __init__(self, rows, cols, whole, first, second, done, sems):
        share = whole.shape[0] // rows.size
        mine = lambda p: pl.ds(pl.multiple_of(p * share, 8), share)
        one, two, three = sems
        self.rows, self.cols, self.mine = rows, cols, mine
        self.whole, self.first, self.second, self.done = whole, first, second, done
        self.one = Exchange(rows, lambda p: whole.at[mine(p)], lambda s: first.at[s], one)
        self.two = Exchange(cols, lambda p: second.at[cols.me], lambda s: second.at[s], two)
        self.three = Exchange(
            rows, lambda p: done.at[mine(rows.me)], lambda s: done.at[mine(s)], three
        )

    def start(self):
        self.first[self.rows.me] = self.whole[self.mine(self.rows.me), :]
        self.one.start()

    def turn(self):
        self.one.wait_recv()
        self.second[self.cols.me] = sum_slots(self.first, self.rows.size)
        self.two.start()

    def back(self):
        self.two.wait_recv()
        self.done[self.mine(self.rows.me), :] = sum_slots(self.second, self.cols.size)
        self.three.start()

    def finish(self):
        self.three.wait_recv()
        for e in (self.one, self.two, self.three):
            e.wait_send()


def last_kernel(
    n_row, n_col, node_count, ortho_ref, residual_ref, p_ref, image_x_ref, image_p_ref,
    rr_ref, rc_ref, image_r_ref, early_ref, late_ref,
    first_in, second_in, second_out, inbox, basis, image_x, image_p,
    e_whole, e_first, e_second, e_done, l_whole, l_first, l_second, l_done,
    s1, s2, s_row, e1, e2, e3, l1, l2, l3, own, loads,
):
    rows, cols = Line("row", n_row), Line("col", n_col)
    plane = Plane(cols)
    k_width, mine = ortho_ref.shape
    blocks = mine // TILE
    sources = [(r, basis.at[pl.ds(i * k_width, k_width)]) for i, r in enumerate((ortho_ref, residual_ref, p_ref))]
    sources += [(image_x_ref, image_x), (image_p_ref, image_p)]
    fetched = [pltpu.make_async_copy(r, to, loads.at[i]) for i, (r, to) in enumerate(sources)]
    for c in fetched:
        c.start()
    greet(rows, cols)
    meet(rows, cols)
    across = PlaneSum(plane, rr_ref, first_in, second_in, second_out, s1, s2, own)
    along = RowSum(rows, rc_ref, inbox, s_row, own.at[2])
    across.start()
    along.start()
    for c in fetched:
        c.wait()
    e_whole[:, : 3 * k_width] = dot_nt(basis[...], basis[...]) / node_count
    e_whole[:, 3 * k_width :] = dot_nt(basis[...], image_x[...]) / node_count
    early = Spread(rows, cols, e_whole, e_first, e_second, e_done, (e1, e2, e3))
    late = Spread(rows, cols, l_whole, l_first, l_second, l_done, (l1, l2, l3))
    early.start()
    from_p = dot_nt(basis[...], image_p[...]) / node_count
    across.pass_on(k_width)
    early.turn()
    from_rows = along.finish(blocks, k_width)
    images = add_lists([across.finish(k_width), from_rows])
    image_r = jnp.concatenate(images, axis=1)
    image_r_ref[...] = image_r
    from_r = dot_nt(basis[...], image_r) / node_count
    l_whole[...] = jnp.concatenate([from_r, from_p], axis=1)
    late.start()
    late.turn()
    early.back()
    late.back()
    early.finish()
    early_ref[...] = e_done[...]
    late.finish()
    late_ref[...] = l_done[...]
    across.wait_send()
    along.wait_send()


def hand_kernel(
    residual_in, image_in, early_ref, late_ref, residual_ref, image_ref, a_ref, b_ref,
    early, late, sems,
):
    pairs = ((early_ref, early), (late_ref, late), (residual_in, residual_ref), (image_in, image_ref))
    copies = [pltpu.make_async_copy(r, to, sems.at[i]) for i, (r, to) in enumerate(pairs)]
    for c in copies:
        c.start()
    full = early.shape[0]
    copies[0].wait()
    copies[1].wait()
    a_ref[...] = jnp.concatenate([early[:, full:], late[...]], axis=1)
    b_ref[...] = early[:, :full]
    copies[2].wait()
    copies[3].wait()


def per_device(block_x, block_p, tile_rows, tile_cols, tile_count, tile_vals):
    n_row, n_col = lax.axis_size("row"), lax.axis_size("col")
    k_width, mine = block_x.shape
    node_count = mine * n_row * n_col
    blocks = mine // TILE
    slots = tile_vals.shape[2]
    vals = tile_vals.reshape(slots, TILE, TILE)
    keep = lambda v: pltpu.with_memory_space_constraint(v, pltpu.HBM)
    tile_rows, tile_cols, vals = keep(tile_rows), keep(tile_cols), keep(vals)
    vmem = pl.BlockSpec(memory_space=pltpu.VMEM)
    anywhere = pl.BlockSpec(memory_space=pl.ANY)
    in_hbm = pl.BlockSpec(memory_space=pltpu.HBM)
    row_sems = pltpu.SemaphoreType.DMA((2, n_row))
    col_sems = pltpu.SemaphoreType.DMA((2, n_col))
    plane_sems = pltpu.SemaphoreType.DMA((2, 2, SIDE, SIDE))
    ring_sems = pltpu.SemaphoreType.DMA((2, 2, SIDE))
    shape = jax.ShapeDtypeStruct
    params = lambda i, mib: pltpu.CompilerParams(
        collective_id=i, has_side_effects=True, vmem_limit_bytes=mib * 2**20
    )
    local = shape((k_width, mine), F32)
    half_rows, all_rows = HALF * k_width + SPARE, blocks * k_width + SPARE
    sum_boxes = [
        pltpu.VMEM((2, SIDE, SIDE, half_rows, TILE), jnp.int16),
        pltpu.VMEM((2, SIDE, half_rows, TILE), jnp.int16),
        pltpu.VMEM((2, SIDE, half_rows, TILE), jnp.int16),
        pltpu.VMEM((n_row, all_rows, TILE), jnp.int16),
    ]
    small = [
        pltpu.VMEM((n_row, k_width // 2, 2 * k_width), F32),
        pltpu.VMEM((n_col, k_width // 2, 2 * k_width), F32),
    ]

    ortho, vrow, vcol = pl.pallas_call(
        functools.partial(first_kernel, n_row, n_col, node_count),
        in_specs=[in_hbm] * 2,
        out_specs=[vmem, anywhere, anywhere],
        out_shape=[
            local,
            shape((n_col, blocks, 2 * k_width, TILE), BF16),
            shape((n_row, blocks, 2 * k_width, TILE), BF16),
        ],
        scratch_shapes=[
            pltpu.VMEM((blocks, 2 * k_width, TILE), BF16),
            pltpu.VMEM((k_width, mine), F32),
            pltpu.VMEM((k_width, mine), F32),
            *small,
            row_sems, col_sems, row_sems, plane_sems, row_sems, plane_sems,
            pltpu.SemaphoreType.DMA((2,)),
            pltpu.SemaphoreType.DMA((2,)),
        ],
        compiler_params=params(0, 8),
    )(keep(block_x), keep(block_p))

    xr, xc, pr, pc = apply_graph(tile_rows, tile_cols, tile_count, vrow, vcol, vals, k_width)

    residual, image_x, image_p, vrow, vcol = pl.pallas_call(
        functools.partial(middle_kernel, n_row, n_col, node_count),
        in_specs=[anywhere] * 5,
        out_specs=[vmem] * 3 + [anywhere] * 2,
        out_shape=[
            local, local, local,
            shape((n_col, blocks, k_width, TILE), BF16),
            shape((n_row, blocks, k_width, TILE), BF16),
        ],
        scratch_shapes=[
            *sum_boxes,
            pltpu.VMEM((2, SIDE, SIDE, HALF * k_width, TILE), BF16),
            pltpu.VMEM((2, SIDE, HALF * k_width, TILE), BF16),
            pltpu.VMEM((2, SIDE, HALF * k_width, TILE), BF16),
            pltpu.VMEM((n_row, blocks * k_width, TILE), BF16),
            pltpu.VMEM((k_width, mine), F32),
            pltpu.VMEM((blocks, k_width, TILE), BF16),
            *small,
            plane_sems, ring_sems, row_sems, plane_sems, ring_sems, row_sems,
            row_sems, col_sems, row_sems, plane_sems,
            pltpu.SemaphoreType.DMA((5,)),
            pltpu.SemaphoreType.DMA((4,)),
        ],
        compiler_params=params(1, 14),
    )(ortho, xr, xc, pr, pc)

    rr, rc = apply_graph(tile_rows, tile_cols, tile_count, vrow, vcol, vals, k_width)

    full = 3 * k_width
    spread = lambda width: [
        pltpu.VMEM((full, width), F32),
        pltpu.VMEM((n_row, full // n_row, width), F32),
        pltpu.VMEM((n_col, full // n_row, width), F32),
        pltpu.VMEM((full, width), F32),
    ]
    image_r, early, late = pl.pallas_call(
        functools.partial(last_kernel, n_row, n_col, node_count),
        in_specs=[anywhere] * 7,
        out_specs=[vmem] * 3,
        out_shape=[local, shape((full, 4 * k_width), F32), shape((full, 2 * k_width), F32)],
        scratch_shapes=[
            *sum_boxes,
            pltpu.VMEM((full, mine), F32),
            pltpu.VMEM((k_width, mine), F32),
            pltpu.VMEM((k_width, mine), F32),
            *spread(4 * k_width), *spread(2 * k_width),
            plane_sems, ring_sems, row_sems,
            row_sems, col_sems, row_sems, row_sems, col_sems, row_sems,
            pltpu.SemaphoreType.DMA((3,)),
            pltpu.SemaphoreType.DMA((5,)),
        ],
        compiler_params=params(2, 12),
    )(ortho, residual, block_p, image_x, image_p, rr, rc)
    return tuple(
        pl.pallas_call(
            hand_kernel,
            in_specs=[anywhere] * 4,
            out_specs=[anywhere] * 2 + [vmem] * 2,
            out_shape=[local, local, shape((full, full), F32), shape((full, full), F32)],
            scratch_shapes=[
                pltpu.VMEM((full, 4 * k_width), F32),
                pltpu.VMEM((full, 2 * k_width), F32),
                pltpu.SemaphoreType.DMA((4,)),
            ],
            compiler_params=pltpu.CompilerParams(vmem_limit_bytes=4 * 2**20),
        )(residual, image_r, early, late)
    )


def solution(mesh):
    in_specs = (
        P(None, ("row", "col")),
        P(None, ("row", "col")),
        P("row", "col", None),
        P("row", "col", None),
        P("row", "col"),
        P("row", "col", None, None, None),
    )
    out_specs = (P(None, ("row", "col")), P(None, ("row", "col")), P(), P())
    return jax.shard_map(
        per_device, mesh=mesh, in_specs=in_specs, out_specs=out_specs, check_vma=False
    )
```

```python
import functools

import jax
import jax.numpy as jnp
from jax import lax
from jax.experimental import pallas as pl
from jax.experimental.pallas import tpu as pltpu
from jax.sharding import PartitionSpec as P

F32 = jnp.float32
BF16 = jnp.bfloat16
TILE = 128
HIGHEST = lax.Precision.HIGHEST
MESH = pl.DeviceIdType.MESH
GROUP = 48
WIDE_GROUP = 96
SIDE = 4
HALF = 3
SPARE = 16
TOP = 32700.0


def dot_nt(left, right):
    return lax.dot_general(
        left, right, (((1,), (1,)), ((), ())), precision=HIGHEST, preferred_element_type=F32
    )


def dot_tn(left, right):
    return lax.dot_general(
        left, right, (((0,), (0,)), ((), ())), precision=HIGHEST, preferred_element_type=F32
    )


def dot_nn(left, right):
    return lax.dot_general(
        left, right, (((1,), (0,)), ((), ())), precision=HIGHEST, preferred_element_type=F32
    )


class Line:
    def __init__(self, name, size):
        self.name, self.size = name, size
        self.me = lax.axis_index(name)

    def ahead(self, k):
        return lax.rem(self.me + k, self.size)

    def behind(self, k):
        return lax.rem(self.me + self.size - k, self.size)

    def greet(self, barrier):
        for k in range(1, self.size):
            pl.semaphore_signal(
                barrier, inc=1, device_id={self.name: self.ahead(k)}, device_id_type=MESH
            )

    def copies(self, source, target, send_sem, recv_sem):
        return [
            pltpu.make_async_remote_copy(
                src_ref=source(self.ahead(k)),
                dst_ref=target(self.me),
                send_sem=send_sem.at[k],
                recv_sem=recv_sem.at[k],
                device_id={self.name: self.ahead(k)},
                device_id_type=MESH,
            )
            for k in range(1, self.size)
        ]

    def arrivals(self, source, target, send_sem, recv_sem):
        return [
            pltpu.make_async_remote_copy(
                src_ref=source(self.ahead(k)),
                dst_ref=target(self.behind(k)),
                send_sem=send_sem.at[k],
                recv_sem=recv_sem.at[k],
                device_id={self.name: self.ahead(k)},
                device_id_type=MESH,
            )
            for k in range(1, self.size)
        ]


class Exchange:
    def __init__(self, line, source, target, sems):
        self.sent = line.copies(source, target, sems.at[0], sems.at[1])
        self.come = line.arrivals(source, target, sems.at[0], sems.at[1])

    def start(self):
        for c in self.sent:
            c.start()
        return self

    def wait_recv(self):
        for c in self.come:
            c.wait_recv()
        return self

    def wait_send(self):
        for c in self.sent:
            c.wait_send()
        return self


def pack(parts, ref):
    width = parts[0].shape[0]
    if ref.dtype == BF16:
        for i, part in enumerate(parts):
            ref[i * width : (i + 1) * width, :] = part.astype(BF16)
        return
    most = jnp.abs(parts[0])
    for part in parts[1:]:
        most = jnp.maximum(most, jnp.abs(part))
    most = jnp.maximum(jnp.max(most, axis=1, keepdims=True), 1e-30)
    power = jnp.clip(jnp.ceil(jnp.log2(most)), -100.0, 126.0)
    up = jnp.exp2(-power) * TOP
    for i, part in enumerate(parts):
        ref[i * width : (i + 1) * width, :] = jnp.round(part * up).astype(jnp.int32).astype(jnp.int16)
    down = lax.broadcasted_iota(jnp.int32, (width, TILE), 0)
    across = lax.broadcasted_iota(jnp.int32, (width, TILE), 1)
    line = jnp.sum(jnp.where(down == across, power, 0.0), axis=0, keepdims=True)
    line = jnp.broadcast_to(line, (SPARE, TILE))
    ref[len(parts) * width :, :] = line.astype(jnp.int32).astype(jnp.int16)


def unpack(ref, count, width):
    if ref.dtype == BF16:
        return [ref[i * width : (i + 1) * width, :].astype(F32) for i in range(count)]
    line = ref[count * width :, :].astype(jnp.int32).astype(F32)[:1]
    down = lax.broadcasted_iota(jnp.int32, (width, TILE), 0)
    across = lax.broadcasted_iota(jnp.int32, (width, TILE), 1)
    power = jnp.sum(jnp.where(down == across, line, 0.0), axis=1, keepdims=True)
    step = jnp.exp2(power) * (1.0 / TOP)
    return [
        ref[i * width : (i + 1) * width, :].astype(jnp.int32).astype(F32) * step
        for i in range(count)
    ]


def add_lists(lists):
    return [functools.reduce(lambda a, b: a + b, parts) for parts in zip(*lists)]


class Plane:
    def __init__(self, cols):
        self.spot = (cols.me // SIDE, lax.rem(cols.me, SIDE))

    def axes(self, half):
        return (self.spot[0], self.spot[1]) if half == 0 else (self.spot[1], self.spot[0])

    def index(self, half, first, second):
        first, second = lax.rem(first, SIDE), lax.rem(second, SIDE)
        return first * SIDE + second if half == 0 else second * SIDE + first

    def copy(self, source, target, sems, at, device):
        return pltpu.make_async_remote_copy(
            src_ref=source,
            dst_ref=target,
            send_sem=sems.at[(0, *at)],
            recv_sem=sems.at[(1, *at)],
            device_id={"col": device},
            device_id_type=MESH,
        )


class PlaneGather:
    def __init__(self, plane, mine, slot, sems):
        self.plane, self.mine, self.slot, self.sems = plane, mine, slot, sems
        self.sent = []

    def send(self, source, owner, half, at, device):
        c = self.plane.copy(source, self.slot(owner, half), self.sems, at, device)
        c.start()
        self.sent.append(c)

    def arrived(self, owner, half, at):
        _, device = self.place(half, 1, 0)
        self.plane.copy(self.mine(half), self.slot(owner, half), self.sems, at, device).wait_recv()

    def place(self, half, first, second):
        f, s = self.plane.axes(half)
        return (
            self.plane.index(half, f + SIDE - first, s + SIDE - second),
            self.plane.index(half, f + first, s + second),
        )

    def start(self):
        for half in (0, 1):
            me, _ = self.place(half, 0, 0)
            for k in range(1, SIDE):
                self.send(self.mine(half), me, half, (half, k, 0), self.place(half, k, 0)[1])
        for half in (0, 1):
            me, _ = self.place(half, 0, 0)
            for k in range(1, SIDE):
                self.send(self.mine(half), me, half, (half, 0, k), self.place(half, 0, k)[1])

    def forward(self):
        for i in (1, 3, 2):
            for half in (0, 1):
                owner, _ = self.place(half, i, 0)
                self.arrived(owner, half, (half, i, 0))
                for k in range(1, SIDE):
                    self.send(
                        self.slot(owner, half), owner, half, (half, i, k), self.place(half, 0, k)[1]
                    )

    def wait_recv(self):
        for i in range(SIDE):
            for k in range(1, SIDE):
                for half in (0, 1):
                    self.arrived(self.place(half, i, k)[0], half, (half, i, k))

    def wait_send(self):
        for c in self.sent:
            c.wait_send()


class PlaneSum:
    def __init__(self, plane, packed, first_in, second_in, second_out, sems1, sems2, own):
        self.plane, self.packed = plane, packed
        self.first_in, self.second_in, self.second_out = first_in, second_in, second_out
        self.sems1, self.sems2 = sems1, sems2
        self.own = [
            pltpu.make_async_copy(
                packed.at[h, pl.ds(plane.axes(h)[0] * SIDE, SIDE)], first_in.at[h, 0], own.at[h]
            )
            for h in (0, 1)
        ]
        self.sent = []

    def hop(self, half, k, j):
        f, s = self.plane.axes(half)
        return self.plane.copy(
            self.packed.at[half, lax.rem(f + k, SIDE) * SIDE + j],
            self.first_in.at[half, k, j],
            self.sems1,
            (half, k, j),
            self.plane.index(half, f + k, s),
        )

    def hop2(self, half, k):
        f, s = self.plane.axes(half)
        return self.plane.copy(
            self.second_out.at[half, k],
            self.second_in.at[half, k],
            self.sems2,
            (half, k),
            self.plane.index(half, f, s + k),
        )

    def start(self):
        for n in (2, 1, 3, 0):
            for half in (0, 1):
                for k in (2, 1, 3):
                    c = self.hop(half, k, self.turn(half, n))
                    c.start()
                    self.sent.append(c)
        for c in self.own:
            c.start()

    def turn(self, half, n):
        return lax.rem(self.plane.axes(half)[1] + n, SIDE)

    def gathered(self, half, k, width):
        j = self.turn(half, k)
        for i in range(1, SIDE):
            self.hop(half, i, j).wait_recv()
        return add_lists(
            [unpack(self.first_in.at[half, i, j], HALF, width) for i in range(SIDE)]
        )

    def pass_on(self, width):
        for c in self.own:
            c.wait()
        for k in (2, 1, 3):
            for half in (0, 1):
                pack(self.gathered(half, k, width), self.second_out.at[half, k])
                c = self.hop2(half, k)
                c.start()
                self.sent.append(c)

    def finish(self, width):
        mine = [self.gathered(half, 0, width) for half in (0, 1)]
        blocks = []
        for half in (0, 1):
            parts = [mine[half]]
            for k in (2, 1, 3):
                self.hop2(half, k).wait_recv()
                parts.append(unpack(self.second_in.at[half, k], HALF, width))
            blocks += add_lists(parts)
        return blocks

    def wait_send(self):
        for c in self.sent:
            c.wait_send()


class RowSum:
    def __init__(self, rows, packed, inbox, sems, own):
        self.rows, self.inbox = rows, inbox
        self.move = Exchange(rows, lambda p: packed.at[p], lambda s: inbox.at[s], sems)
        self.own = pltpu.make_async_copy(packed.at[rows.me], inbox.at[rows.me], own)

    def start(self):
        self.move.start()
        self.own.start()

    def finish(self, count, width):
        self.own.wait()
        self.move.wait_recv()
        return add_lists([unpack(self.inbox.at[j], count, width) for j in range(self.rows.size)])

    def wait_send(self):
        self.move.wait_send()


def greet(rows, cols):
    barrier = pltpu.get_barrier_semaphore()
    rows.greet(barrier)
    cols.greet(barrier)


def meet(rows, cols):
    pl.semaphore_wait(pltpu.get_barrier_semaphore(), rows.size + cols.size - 2)


def sum_slots(ref, count):
    total = ref[0]
    for j in range(1, count):
        total = total + ref[j]
    return total


def all_reduce(
    rows, cols, part, first, second, row_sems, col_sems, between=None, before=None
):
    half = part.shape[0] // 2
    first[rows.me] = jnp.concatenate([part[:half], part[half:]], axis=1)
    one = Exchange(rows, lambda p: first.at[rows.me], lambda s: first.at[s], row_sems)
    one.start()
    if before is not None:
        before()
    one.wait_recv()
    second[cols.me] = sum_slots(first, rows.size)
    two = Exchange(cols, lambda p: second.at[cols.me], lambda s: second.at[s], col_sems)
    two.start()
    if between is not None:
        between()
    two.wait_recv()
    total = sum_slots(second, cols.size)
    one.wait_send()
    two.wait_send()
    return jnp.concatenate([total[:, : 2 * half], total[:, 2 * half :]], axis=0)


def factor(gram):
    k_width = gram.shape[0]
    row_id = lax.broadcasted_iota(jnp.int32, (k_width, k_width), 0)
    col_id = lax.broadcasted_iota(jnp.int32, (k_width, k_width), 1)
    eye = jnp.where(row_id == col_id, 1.0, 0.0).astype(F32)
    work = jnp.concatenate([gram, eye], axis=1)
    down = lax.broadcasted_iota(jnp.int32, (k_width, 2 * k_width), 0)
    pivots = []
    for k in range(k_width):
        pivot_row = work[k : k + 1, :]
        pivot = work[k : k + 1, k : k + 1]
        pivots.append(pivot)
        if k + 1 < k_width:
            ratio = work[:, k : k + 1]
            work = work - jnp.where(down > k, ratio * (pivot_row * (1.0 / pivot)), 0.0)
    scale = lax.rsqrt(jnp.concatenate(pivots, axis=0))
    return work[:, k_width:] * scale


def first_kernel(
    n_row, n_col, node_count, x_ref, p_ref, ortho_ref, vrow_ref, vcol_ref,
    low, x, p, first, second, ar_row, ar_col, p_row, p_plane, x_row, x_plane, own, loads,
):
    rows, cols = Line("row", n_row), Line("col", n_col)
    plane = Plane(cols)
    k_width, mine = x_ref.shape
    blocks = mine // TILE
    fetched = [
        pltpu.make_async_copy(ref, to, loads.at[i]) for i, (ref, to) in enumerate(((x_ref, x), (p_ref, p)))
    ]
    for c in fetched:
        c.start()
    greet(rows, cols)
    fetched[0].wait()
    part = dot_nt(x[...], x[...]) / node_count
    fetched[1].wait()
    for b in range(blocks):
        low[b, k_width:, :] = p[:, b * TILE : (b + 1) * TILE].astype(BF16)
    meet(rows, cols)

    def gathers(band, row_sems, plane_sems):
        across = PlaneGather(
            plane,
            lambda h: low.at[pl.ds(h * HALF, HALF), band, :],
            lambda owner, h: vrow_ref.at[owner, pl.ds(h * HALF, HALF), band, :],
            plane_sems,
        )
        along = Exchange(
            rows, lambda p: low.at[:, band, :], lambda s: vcol_ref.at[s, :, band, :], row_sems
        )
        return across, along

    p_across, p_along = gathers(pl.ds(k_width, k_width), p_row, p_plane)
    x_across, x_along = gathers(pl.ds(0, k_width), x_row, x_plane)

    def pass_p():
        p_across.forward()
        p_along.start()

    gram = all_reduce(
        rows, cols, part, first, second, ar_row, ar_col, pass_p, p_across.start
    )
    ortho = dot_nn(factor(gram), x[...])
    ortho_ref[...] = ortho
    for b in range(blocks):
        low[b, :k_width, :] = ortho[:, b * TILE : (b + 1) * TILE].astype(BF16)
    x_across.start()
    x_along.start()
    here = [
        pltpu.make_async_copy(low, vrow_ref.at[cols.me], own.at[0]),
        pltpu.make_async_copy(low, vcol_ref.at[rows.me], own.at[1]),
    ]
    for c in here:
        c.start()
    x_across.forward()
    moves = (p_across, p_along, x_across, x_along)
    for m in moves:
        m.wait_recv()
    for m in moves:
        m.wait_send()
    for c in here:
        c.wait()


def times(left, right, right_dim):
    return lax.dot_general(
        left, right, (((1,), (right_dim,)), ((), ())), preferred_element_type=F32
    )


def apply_kernel(
    k_width, rows_in, cols_in, count_ref, vrow, vcol, tile_ref, *rest
):
    n_out = (len(rest) - 8) // 2
    outs, boxes = rest[:n_out], rest[n_out : 2 * n_out]
    rows_ref, cols_ref, tiles, row_acc, col_acc, tile_sems, in_sems, out_sems = rest[2 * n_out :]
    row_blocks, width, _ = vrow.shape
    col_blocks = vcol.shape[0]
    count = count_ref[0, 0]
    size = tiles.shape[0] // tile_sems.shape[0]
    groups = (count + size - 1) // size

    def tile_copy(g):
        part = pl.ds(g * size, size)
        return pltpu.make_async_copy(tile_ref.at[part], tiles.at[part], tile_sems.at[g])

    def start_copy(g, carry):
        tile_copy(g).start()
        return carry

    inputs = [
        pltpu.make_async_copy(rows_in, rows_ref, in_sems.at[0]),
        pltpu.make_async_copy(cols_in, cols_ref, in_sems.at[1]),
    ]
    for c in inputs:
        c.start()
    tile_copy(0).start()
    lax.fori_loop(1, groups, start_copy, 0)
    row_acc[...] = jnp.zeros_like(row_acc)
    col_acc[...] = jnp.zeros_like(col_acc)
    for c in inputs:
        c.wait()

    def place(slot):
        live = slot < count
        a, b = rows_ref[0, 0, slot], cols_ref[0, 0, slot]
        return a, b, jnp.where(live, a, row_blocks), jnp.where(live, b, col_blocks)

    def single(slot):
        a, b, to_row, to_col = place(slot)
        tile = tiles[slot]
        row_acc[to_row] += times(vcol[b], tile, 1)
        col_acc[to_col] += times(vrow[a], tile, 0)

    def pair(slot):
        a, b, to_row, to_col = place(slot)
        a2, b2, to_row2, to_col2 = place(slot + 1)
        tile, tile2 = tiles[slot], tiles[slot + 1]
        none = jnp.zeros((width, TILE), BF16)

        def beside(u, v):
            return jnp.concatenate(
                [jnp.concatenate([u, none], axis=1), jnp.concatenate([none, v], axis=1)], axis=0
            )

        forward = times(beside(vcol[b], vcol[b2]), jnp.concatenate([tile, tile2], axis=1), 1)
        row_acc[to_row] += forward[:width]
        row_acc[to_row2] += forward[width:]
        backward = times(beside(vrow[a], vrow[a2]), jnp.concatenate([tile, tile2], axis=0), 0)
        col_acc[to_col] += backward[:width]
        col_acc[to_col2] += backward[width:]

    def group(g, carry):
        tile_copy(g).wait()
        if width < TILE:
            for u in range(0, size, 2):
                pair(g * size + u)
        else:
            for u in range(size):
                single(g * size + u)
        return carry

    lax.fori_loop(0, groups, group, 0)

    n_row, n_col = boxes[1].shape[0], boxes[0].shape[1]
    blocks = row_blocks // n_col
    results = [
        pltpu.make_async_copy(box, out, out_sems.at[i]) for i, (box, out) in enumerate(zip(boxes, outs))
    ]
    for i in range(n_out - 2, -1, -2):
        band = pl.ds(i // 2 * k_width, k_width)

        def pack_row(c, carry):
            for half in (0, 1):
                at = c if half == 0 else lax.rem(c, SIDE) * SIDE + c // SIDE
                parts = [row_acc[c * blocks + half * HALF + n, band, :] for n in range(HALF)]
                pack(parts, boxes[i].at[half, at])
            return carry

        def pack_col(r, carry):
            pack([col_acc[r * blocks + n, band, :] for n in range(blocks)], boxes[i + 1].at[r])
            return carry

        lax.fori_loop(0, n_col, pack_row, 0)
        results[i].start()
        lax.fori_loop(0, n_row, pack_col, 0)
        results[i + 1].start()
    for c in results:
        c.wait()


def apply_graph(tile_rows, tile_cols, count, vrow, vcol, vals, k_width):
    n_col, blocks, width, _ = vrow.shape
    n_row = vcol.shape[0]
    slots = vals.shape[0]
    row_blocks, col_blocks = n_col * blocks, n_row * blocks
    smem = pl.BlockSpec(memory_space=pltpu.SMEM)
    vmem = pl.BlockSpec(memory_space=pltpu.VMEM)
    near = lambda v: pltpu.with_memory_space_constraint(v, pltpu.VMEM)
    in_hbm = pl.BlockSpec(memory_space=pltpu.HBM)
    anywhere = pl.BlockSpec(memory_space=pl.ANY)
    shape = jax.ShapeDtypeStruct
    out_shape = [
        shape((2, n_col, HALF * k_width + SPARE, TILE), jnp.int16),
        shape((n_row, blocks * k_width + SPARE, TILE), jnp.int16),
    ]
    if width > k_width:
        out_shape += [
            shape((2, n_col, HALF * k_width, TILE), BF16),
            shape((n_row, blocks * k_width, TILE), BF16),
        ]
    return pl.pallas_call(
        functools.partial(apply_kernel, k_width),
        in_specs=[in_hbm] * 2 + [smem] + [vmem] * 2 + [in_hbm],
        out_specs=[anywhere] * len(out_shape),
        out_shape=out_shape,
        scratch_shapes=[
            *[pltpu.VMEM(o.shape, o.dtype) for o in out_shape],
            pltpu.SMEM(tile_rows.shape, jnp.int32),
            pltpu.SMEM(tile_cols.shape, jnp.int32),
            pltpu.VMEM((slots, TILE, TILE), BF16),
            pltpu.VMEM((row_blocks + 1, width, TILE), F32),
            pltpu.VMEM((col_blocks + 1, width, TILE), F32),
            pltpu.SemaphoreType.DMA((slots // (GROUP if width == TILE else WIDE_GROUP),)),
            pltpu.SemaphoreType.DMA((2,)),
            pltpu.SemaphoreType.DMA((len(out_shape),)),
        ],
        compiler_params=pltpu.CompilerParams(vmem_limit_bytes=(24 + 18 * width // TILE) * 2**20),
        cost_estimate=pl.CostEstimate(
            flops=16 * slots * width * TILE * TILE,
            bytes_accessed=2 * slots * TILE * TILE,
            transcendentals=0,
        ),
    )(
        tile_rows, tile_cols, count,
        near(vrow.reshape(row_blocks, width, TILE)),
        near(vcol.reshape(col_blocks, width, TILE)),
        vals,
    )


def middle_kernel(
    n_row, n_col, node_count, ortho_ref, xr_ref, xc_ref, pr_ref, pc_ref,
    residual_ref, image_x_ref, image_p_ref, vrow_ref, vcol_ref,
    first_in, second_in, second_out, inbox, p_first_in, p_second_in, p_second_out, p_inbox,
    ortho, low, first, second,
    s1, s2, s_row, p1, p2, p_row, ar_row, ar_col, g_row, g_plane, own, loads,
):
    rows, cols = Line("row", n_row), Line("col", n_col)
    plane = Plane(cols)
    k_width, mine = ortho_ref.shape
    blocks = mine // TILE
    fetched = pltpu.make_async_copy(ortho_ref, ortho, loads.at[0])
    fetched.start()
    greet(rows, cols)
    meet(rows, cols)
    across = PlaneSum(plane, xr_ref, first_in, second_in, second_out, s1, s2, own)
    along = RowSum(rows, xc_ref, inbox, s_row, own.at[2])
    p_across = PlaneSum(plane, pr_ref, p_first_in, p_second_in, p_second_out, p1, p2, loads.at[pl.ds(1, 2)])
    p_along = RowSum(rows, pc_ref, p_inbox, p_row, loads.at[3])
    across.start()
    along.start()
    across.pass_on(k_width)
    p_across.start()
    from_rows = along.finish(blocks, k_width)
    images = add_lists([across.finish(k_width), from_rows])
    image_x_ref[...] = jnp.concatenate(images, axis=1)
    fetched.wait()
    part = dot_nt(ortho[...], image_x_ref[...]) / node_count

    def meanwhile():
        p_across.pass_on(k_width)
        p_along.start()

    rayleigh = all_reduce(rows, cols, part, first, second, ar_row, ar_col, meanwhile)
    residual = image_x_ref[...] - dot_tn(rayleigh, ortho[...])
    residual_ref[...] = residual
    for b in range(blocks):
        low[b] = residual[:, b * TILE : (b + 1) * TILE].astype(BF16)
    g_across = PlaneGather(
        plane,
        lambda h: low.at[pl.ds(h * HALF, HALF)],
        lambda owner, h: vrow_ref.at[owner, pl.ds(h * HALF, HALF)],
        g_plane,
    )
    g_along = Exchange(rows, lambda p: low, lambda s: vcol_ref.at[s], g_row)
    g_across.start()
    g_along.start()
    here = [
        pltpu.make_async_copy(low, vrow_ref.at[cols.me], own.at[3]),
        pltpu.make_async_copy(low, vcol_ref.at[rows.me], own.at[4]),
    ]
    for c in here:
        c.start()
    g_across.forward()
    p_images = add_lists([p_across.finish(k_width), p_along.finish(blocks, k_width)])
    image_p_ref[...] = jnp.concatenate(p_images, axis=1)
    g_across.wait_recv()
    g_along.wait_recv()
    for c in here:
        c.wait()
    for c in (across, along, p_across, p_along, g_across, g_along):
        c.wait_send()


class Spread:
    def __init__(self, rows, cols, whole, first, second, done, sems):
        share = whole.shape[0] // rows.size
        mine = lambda p: pl.ds(pl.multiple_of(p * share, 8), share)
        one, two, three = sems
        self.rows, self.cols, self.mine = rows, cols, mine
        self.whole, self.first, self.second, self.done = whole, first, second, done
        self.one = Exchange(rows, lambda p: whole.at[mine(p)], lambda s: first.at[s], one)
        self.two = Exchange(cols, lambda p: second.at[cols.me], lambda s: second.at[s], two)
        self.three = Exchange(
            rows, lambda p: done.at[mine(rows.me)], lambda s: done.at[mine(s)], three
        )

    def start(self):
        self.first[self.rows.me] = self.whole[self.mine(self.rows.me), :]
        self.one.start()

    def turn(self):
        self.one.wait_recv()
        self.second[self.cols.me] = sum_slots(self.first, self.rows.size)
        self.two.start()

    def back(self):
        self.two.wait_recv()
        self.done[self.mine(self.rows.me), :] = sum_slots(self.second, self.cols.size)
        self.three.start()

    def finish(self):
        self.three.wait_recv()
        for e in (self.one, self.two, self.three):
            e.wait_send()


def last_kernel(
    n_row, n_col, node_count, ortho_ref, residual_ref, p_ref, image_x_ref, image_p_ref,
    rr_ref, rc_ref, image_r_ref, early_ref, late_ref,
    first_in, second_in, second_out, inbox, basis, image_x, image_p,
    e_whole, e_first, e_second, e_done, l_whole, l_first, l_second, l_done,
    s1, s2, s_row, e1, e2, e3, l1, l2, l3, own, loads,
):
    rows, cols = Line("row", n_row), Line("col", n_col)
    plane = Plane(cols)
    k_width, mine = ortho_ref.shape
    blocks = mine // TILE
    sources = [(r, basis.at[pl.ds(i * k_width, k_width)]) for i, r in enumerate((ortho_ref, residual_ref, p_ref))]
    sources += [(image_x_ref, image_x), (image_p_ref, image_p)]
    fetched = [pltpu.make_async_copy(r, to, loads.at[i]) for i, (r, to) in enumerate(sources)]
    for c in fetched:
        c.start()
    greet(rows, cols)
    meet(rows, cols)
    across = PlaneSum(plane, rr_ref, first_in, second_in, second_out, s1, s2, own)
    along = RowSum(rows, rc_ref, inbox, s_row, own.at[2])
    across.start()
    along.start()
    for c in fetched:
        c.wait()
    e_whole[:, : 3 * k_width] = dot_nt(basis[...], basis[...]) / node_count
    e_whole[:, 3 * k_width :] = dot_nt(basis[...], image_x[...]) / node_count
    early = Spread(rows, cols, e_whole, e_first, e_second, e_done, (e1, e2, e3))
    late = Spread(rows, cols, l_whole, l_first, l_second, l_done, (l1, l2, l3))
    early.start()
    from_p = dot_nt(basis[...], image_p[...]) / node_count
    across.pass_on(k_width)
    early.turn()
    from_rows = along.finish(blocks, k_width)
    images = add_lists([across.finish(k_width), from_rows])
    image_r = jnp.concatenate(images, axis=1)
    image_r_ref[...] = image_r
    from_r = dot_nt(basis[...], image_r) / node_count
    l_whole[...] = jnp.concatenate([from_r, from_p], axis=1)
    late.start()
    late.turn()
    early.back()
    late.back()
    early.finish()
    early_ref[...] = e_done[...]
    late.finish()
    late_ref[...] = l_done[...]
    across.wait_send()
    along.wait_send()


def hand_kernel(
    residual_in, image_in, early_ref, late_ref, residual_ref, image_ref, a_ref, b_ref,
    early, late, sems,
):
    pairs = ((early_ref, early), (late_ref, late), (residual_in, residual_ref), (image_in, image_ref))
    copies = [pltpu.make_async_copy(r, to, sems.at[i]) for i, (r, to) in enumerate(pairs)]
    for c in copies:
        c.start()
    full = early.shape[0]
    copies[0].wait()
    copies[1].wait()
    a_ref[...] = jnp.concatenate([early[:, full:], late[...]], axis=1)
    b_ref[...] = early[:, :full]
    copies[2].wait()
    copies[3].wait()


def per_device(block_x, block_p, tile_rows, tile_cols, tile_count, tile_vals):
    n_row, n_col = lax.axis_size("row"), lax.axis_size("col")
    k_width, mine = block_x.shape
    node_count = mine * n_row * n_col
    blocks = mine // TILE
    slots = tile_vals.shape[2]
    vals = tile_vals.reshape(slots, TILE, TILE)
    keep = lambda v: pltpu.with_memory_space_constraint(v, pltpu.HBM)
    tile_rows, tile_cols, vals = keep(tile_rows), keep(tile_cols), keep(vals)
    vmem = pl.BlockSpec(memory_space=pltpu.VMEM)
    anywhere = pl.BlockSpec(memory_space=pl.ANY)
    in_hbm = pl.BlockSpec(memory_space=pltpu.HBM)
    row_sems = pltpu.SemaphoreType.DMA((2, n_row))
    col_sems = pltpu.SemaphoreType.DMA((2, n_col))
    plane_sems = pltpu.SemaphoreType.DMA((2, 2, SIDE, SIDE))
    ring_sems = pltpu.SemaphoreType.DMA((2, 2, SIDE))
    shape = jax.ShapeDtypeStruct
    params = lambda i, mib: pltpu.CompilerParams(
        collective_id=i, has_side_effects=True, vmem_limit_bytes=mib * 2**20
    )
    local = shape((k_width, mine), F32)
    half_rows, all_rows = HALF * k_width + SPARE, blocks * k_width + SPARE
    sum_boxes = [
        pltpu.VMEM((2, SIDE, SIDE, half_rows, TILE), jnp.int16),
        pltpu.VMEM((2, SIDE, half_rows, TILE), jnp.int16),
        pltpu.VMEM((2, SIDE, half_rows, TILE), jnp.int16),
        pltpu.VMEM((n_row, all_rows, TILE), jnp.int16),
    ]
    small = [
        pltpu.VMEM((n_row, k_width // 2, 2 * k_width), F32),
        pltpu.VMEM((n_col, k_width // 2, 2 * k_width), F32),
    ]

    ortho, vrow, vcol = pl.pallas_call(
        functools.partial(first_kernel, n_row, n_col, node_count),
        in_specs=[in_hbm] * 2,
        out_specs=[vmem, anywhere, anywhere],
        out_shape=[
            local,
            shape((n_col, blocks, 2 * k_width, TILE), BF16),
            shape((n_row, blocks, 2 * k_width, TILE), BF16),
        ],
        scratch_shapes=[
            pltpu.VMEM((blocks, 2 * k_width, TILE), BF16),
            pltpu.VMEM((k_width, mine), F32),
            pltpu.VMEM((k_width, mine), F32),
            *small,
            row_sems, col_sems, row_sems, plane_sems, row_sems, plane_sems,
            pltpu.SemaphoreType.DMA((2,)),
            pltpu.SemaphoreType.DMA((2,)),
        ],
        compiler_params=params(0, 8),
    )(keep(block_x), keep(block_p))

    xr, xc, pr, pc = apply_graph(tile_rows, tile_cols, tile_count, vrow, vcol, vals, k_width)

    residual, image_x, image_p, vrow, vcol = pl.pallas_call(
        functools.partial(middle_kernel, n_row, n_col, node_count),
        in_specs=[anywhere] * 5,
        out_specs=[vmem] * 3 + [anywhere] * 2,
        out_shape=[
            local, local, local,
            shape((n_col, blocks, k_width, TILE), BF16),
            shape((n_row, blocks, k_width, TILE), BF16),
        ],
        scratch_shapes=[
            *sum_boxes,
            pltpu.VMEM((2, SIDE, SIDE, HALF * k_width, TILE), BF16),
            pltpu.VMEM((2, SIDE, HALF * k_width, TILE), BF16),
            pltpu.VMEM((2, SIDE, HALF * k_width, TILE), BF16),
            pltpu.VMEM((n_row, blocks * k_width, TILE), BF16),
            pltpu.VMEM((k_width, mine), F32),
            pltpu.VMEM((blocks, k_width, TILE), BF16),
            *small,
            plane_sems, ring_sems, row_sems, plane_sems, ring_sems, row_sems,
            row_sems, col_sems, row_sems, plane_sems,
            pltpu.SemaphoreType.DMA((5,)),
            pltpu.SemaphoreType.DMA((4,)),
        ],
        compiler_params=params(1, 14),
    )(ortho, xr, xc, pr, pc)

    rr, rc = apply_graph(tile_rows, tile_cols, tile_count, vrow, vcol, vals, k_width)

    full = 3 * k_width
    spread = lambda width: [
        pltpu.VMEM((full, width), F32),
        pltpu.VMEM((n_row, full // n_row, width), F32),
        pltpu.VMEM((n_col, full // n_row, width), F32),
        pltpu.VMEM((full, width), F32),
    ]
    image_r, early, late = pl.pallas_call(
        functools.partial(last_kernel, n_row, n_col, node_count),
        in_specs=[anywhere] * 7,
        out_specs=[vmem] * 3,
        out_shape=[local, shape((full, 4 * k_width), F32), shape((full, 2 * k_width), F32)],
        scratch_shapes=[
            *sum_boxes,
            pltpu.VMEM((full, mine), F32),
            pltpu.VMEM((k_width, mine), F32),
            pltpu.VMEM((k_width, mine), F32),
            *spread(4 * k_width), *spread(2 * k_width),
            plane_sems, ring_sems, row_sems,
            row_sems, col_sems, row_sems, row_sems, col_sems, row_sems,
            pltpu.SemaphoreType.DMA((3,)),
            pltpu.SemaphoreType.DMA((5,)),
        ],
        compiler_params=params(2, 12),
    )(ortho, residual, block_p, image_x, image_p, rr, rc)
    return tuple(
        pl.pallas_call(
            hand_kernel,
            in_specs=[anywhere] * 4,
            out_specs=[anywhere] * 2 + [vmem] * 2,
            out_shape=[local, local, shape((full, full), F32), shape((full, full), F32)],
            scratch_shapes=[
                pltpu.VMEM((full, 4 * k_width), F32),
                pltpu.VMEM((full, 2 * k_width), F32),
                pltpu.SemaphoreType.DMA((4,)),
            ],
            compiler_params=pltpu.CompilerParams(vmem_limit_bytes=4 * 2**20),
        )(residual, image_r, early, late)
    )


def solution(mesh):
    in_specs = (
        P(None, ("row", "col")),
        P(None, ("row", "col")),
        P("row", "col", None),
        P("row", "col", None),
        P("row", "col"),
        P("row", "col", None, None, None),
    )
    out_specs = (P(None, ("row", "col")), P(None, ("row", "col")), P(), P())
    return jax.shard_map(
        per_device, mesh=mesh, in_specs=in_specs, out_specs=out_specs, check_vma=False
    )
```
